128 devices in a mesh: section: 2 (over x_hi), dp: 32 (over z, y, x_lo), seq: 2 (over core).
Axes of the slice: x: 4 (x_hi: 2, x_lo: 2; x = x_hi * 2 + x_lo), y: 4, z: 4, core: 2. Of those that a mesh axis runs over, the one named last changes fastest.
Arguments:
- x_in: bfloat16 [32, 4, 128, 3072], P('dp', None, 'seq'), may hold values from -6 to 6
- time_index: int32 [32], P('dp'), may hold values from 0 to 27
- mod_table: float32 [2, 28, 3, 3072], P('section'), may hold values from -3 to 3
- w_qkv: bfloat16 [2, 3072, 16, 3, 128], P('section', 'dp', 'seq'), may hold values from -0.109375 to 0.109375
- w_out: bfloat16 [2, 2048, 3072], P('section', 'dp', 'seq'), may hold values from -0.5 to 0.5
- stale_kv: bfloat16 [2, 32, 512, 2, 16, 128], P('section', 'dp', None, None, 'seq'), may hold values from -6 to 6
Outputs:
- layer_out: bfloat16 [2, 32, 4, 128, 3072], P('section', 'dp', None, 'seq')
- fresh_kv: bfloat16 [2, 32, 512, 2, 16, 128], P('section', 'dp', None, None, 'seq')
The draws below stay inside these ranges and needn't reach their ends.
All inputs are finite; a program needn't handle non-finite values.
Results may differ from the reference program's by a relative error of at most 0.009.
Values may be sent and summed in bfloat16 or wider, within the bound.
A program may use at most 128 MiB of HBM per device.

```python
import math
import jax
import jax.numpy as jnp
from jax import lax

D = 3072
HEADS = 16
HD = 128
TSTEPS = 28
PATCHES = 4
PTOK = 128
INNER = 2048
TOKENS = 512
IMAGES = 32
LAYERS = 2


def place_ends(result, own_key, smallest, largest):
    shape = result.shape
    spot = [jax.random.randint(jax.random.fold_in(own_key, axis), (), 0, shape[axis]) for axis in range(len(shape))]
    result = result.at[tuple(spot)].set(smallest)
    longest = shape.index(max(shape))
    spot[longest] = (spot[longest] + 1) % shape[longest]
    return result.at[tuple(spot)].set(largest)


def level_of(own_key, shape, cuts, low, top_value):
    def one(position, blocks):
        steps = jax.random.uniform(jax.random.fold_in(jax.random.fold_in(own_key, 6), position), (blocks,), jnp.float32, low / len(cuts), top_value / len(cuts))
        return jnp.repeat(jnp.exp(steps), shape[position] // blocks).reshape((-1,) + (1,) * (len(shape) - position - 1))

    gain = one(*cuts[0])
    for cut in cuts[1:]:
        gain = gain * one(*cut)
    return gain


def bell_draw(rng, shape, scale, bound, cuts=(), kind=jnp.bfloat16):
    factor_of = level_of(rng, shape, cuts, -0.22, 0.18) if cuts else 1.0
    entries = jax.random.normal(rng, shape, jnp.float32) * scale * factor_of
    return jnp.minimum(jnp.maximum(entries, -bound), bound).astype(kind)


def setup_inputs(seed: int = 0) -> dict:
    key_of = jax.random.split(jax.random.key(seed), 7)
    x_in = bell_draw(key_of[0], (IMAGES, PATCHES, PTOK, D), 1.0, 6.0, ((0, 32), (2, 2)))
    time_index = place_ends(jax.random.randint(key_of[1], (IMAGES,), 0, TSTEPS), jax.random.fold_in(key_of[1], 1), 0, TSTEPS - 1).astype(jnp.int32)
    mod_table = bell_draw(key_of[2], (LAYERS, TSTEPS, 3, D), 0.6, 3.0, ((0, 2),), jnp.float32)
    w_qkv = bell_draw(key_of[3], (LAYERS, D, HEADS, 3, HD), D ** -0.5, 0.109375, ((0, 2), (1, 32), (2, 2)))
    w_out = bell_draw(key_of[4], (LAYERS, INNER, D), HD ** -0.5, 0.5, ((0, 2), (1, 32), (2, 2)))
    stale_kv = bell_draw(key_of[5], (LAYERS, IMAGES, TOKENS, 2, HEADS, HD), 1.0, 6.0, ((0, 2), (1, 32), (4, 2)))
    return {"x_in": x_in, "time_index": time_index, "mod_table": mod_table, "w_qkv": w_qkv, "w_out": w_out, "stale_kv": stale_kv}


EPS = 1e-06

def qk_norm(values_in):
    return (values_in * lax.rsqrt(lax.optimization_barrier(jnp.mean(jnp.square(values_in), -1, keepdims=True)) + EPS)).astype(jnp.bfloat16)

def reference(x_in, time_index, mod_table, w_qkv, w_out, stale_kv):
    steps_range = jnp.arange(TSTEPS, dtype=jnp.int32)
    onehot = (time_index[:, None] == steps_range[None, :]).astype(jnp.float32)
    hidden = x_in
    layer_list = []
    table_list = []
    for layer in range(LAYERS):
        modulation = jnp.einsum('it,tcd->icd', onehot, mod_table[layer], precision=lax.Precision.HIGHEST)
        shift_vec = modulation[:, 0][:, None, :]
        scale_vec = modulation[:, 1][:, None, :]
        gate_vec = modulation[:, 2][:, None, :]
        proj_in = w_qkv[layer].reshape(D, HEADS * 3 * HD)
        kv_table = stale_kv[layer]
        patch_list = []
        for patch_id in range(PATCHES):
            rows_f32 = hidden[:, patch_id].astype(jnp.float32)
            row_mean = lax.optimization_barrier(jnp.mean(rows_f32, -1, keepdims=True))
            row_var = lax.optimization_barrier(jnp.mean(jnp.square(rows_f32 - row_mean), -1, keepdims=True))
            modulated = ((rows_f32 - row_mean) * lax.rsqrt(row_var + EPS) * (1.0 + scale_vec) + shift_vec).astype(jnp.bfloat16)
            qkv = jnp.dot(modulated.reshape(IMAGES * PTOK, D), proj_in, preferred_element_type=jnp.float32)
            qkv = qkv.reshape(IMAGES, PTOK, HEADS, 3, HD)
            queries = qk_norm(qkv[:, :, :, 0])
            keys_new = qk_norm(qkv[:, :, :, 1])
            values_new = qkv[:, :, :, 2].astype(jnp.bfloat16)
            fresh_rows = jnp.stack((keys_new, values_new), axis=2)
            kv_table = lax.dynamic_update_slice_in_dim(kv_table, fresh_rows, patch_id * PTOK, axis=1)
            scores = jnp.einsum('iqhd,ikhd->ihqk', queries.astype(jnp.float32), kv_table[:, :, 0].astype(jnp.float32)) / math.sqrt(HD)
            exp_scores = jnp.exp(scores)
            probs = (exp_scores / lax.optimization_barrier(jnp.sum(exp_scores, -1, keepdims=True))).astype(jnp.bfloat16)
            mixed_heads = jnp.einsum('ihqk,ikhd->iqhd', probs.astype(jnp.float32), kv_table[:, :, 1].astype(jnp.float32)).astype(jnp.bfloat16)
            attn = jnp.dot(mixed_heads.reshape(IMAGES * PTOK, INNER), w_out[layer], preferred_element_type=jnp.float32)
            attn = attn.astype(jnp.bfloat16).reshape(IMAGES, PTOK, D)
            new_rows = (rows_f32 + gate_vec * attn.astype(jnp.float32)).astype(jnp.bfloat16)
            patch_list.append(new_rows)
        hidden = jnp.stack(patch_list, axis=1)
        layer_list.append(hidden)
        table_list.append(kv_table)
    return (jnp.stack(layer_list), jnp.stack(table_list))
```

```python
import math

import jax
import jax.numpy as jnp
from jax import lax
from jax.experimental import pallas as pl
from jax.experimental.pallas import tpu as pltpu
from jax.sharding import PartitionSpec as P

EPS = 1e-06

MESH = pl.DeviceIdType.MESH
ALL = slice(None)

def place():
    dp = lax.axis_index("dp")
    return lax.div(dp, 8), lax.rem(lax.div(dp, 2), 4), lax.rem(dp, 2)

class Gather:
    def __init__(self, bufs, rows, ssem, rsem):
        self.bufs, self.rows, self.ssem, self.rsem = bufs, rows, ssem, rsem
        self.z, self.y, self.x = place()
    def step(self, v, by):
        return lax.rem(v + (by + 4), 4)
    def view(self, s, part, zs, ys, xs):
        r0, n = self.rows[s][part]
        return self.bufs[s].at[zs, ys, xs, pl.ds(r0, n), :]
    def dev(self, dz=0, dy=0, dx=0):
        z = self.step(self.z, dz) if dz else self.z
        y = self.step(self.y, dy) if dy else self.y
        x = 1 - self.x if dx else self.x
        return {"dp": z * 8 + y * 2 + x}
    def copy(self, s, part, k, sel, to):
        v = self.view(s, part, *sel)
        i = s * 34 + {"A": 0, "B": 9, "C": 18, "D": 26}[part] + k
        return pltpu.make_async_remote_copy(src_ref=v, dst_ref=v, send_sem=self.ssem.at[i], recv_sem=self.rsem.at[i],
            device_id=to, device_id_type=MESH)
    def sel(self, swap, f, g, x):
        return (f, g, x) if swap else (g, f, x)
    def to(self, swap, df=0, dg=0, dx=0):
        return self.dev(dz=df, dy=dg, dx=dx) if swap else self.dev(dz=dg, dy=df, dx=dx)
    def ring(self, swap, second, part):
        f0, g0 = (self.z, self.y) if swap else (self.y, self.z)
        st = self.step
        x = self.x
        out = {}
        if part in "AB":
            out[0] = (self.sel(swap, f0, g0, x), self.sel(swap, f0, g0, 1 - x), self.to(swap, dx=1))
            out[1] = (self.sel(swap, f0, g0, ALL), self.sel(swap, st(f0, -1), g0, ALL), self.to(swap, df=1))
            out[2] = (self.sel(swap, f0, g0, ALL), self.sel(swap, st(f0, 1), g0, ALL), self.to(swap, df=-1))
            out[3] = (self.sel(swap, st(f0, -1), g0, 0), self.sel(swap, st(f0, 2), g0, 0), self.to(swap, df=1))
            out[4] = (self.sel(swap, st(f0, 1), g0, 1), self.sel(swap, st(f0, 2), g0, 1), self.to(swap, df=-1))
            out[5] = (self.sel(swap, ALL, g0, ALL), self.sel(swap, ALL, st(g0, -1), ALL), self.to(swap, dg=1))
            out[6] = (self.sel(swap, ALL, g0, ALL), self.sel(swap, ALL, st(g0, 1), ALL), self.to(swap, dg=-1))
            out[7] = (self.sel(swap, pl.ds(0, 2), st(g0, -1), ALL), self.sel(swap, pl.ds(0, 2), st(g0, 2), ALL), self.to(swap, dg=1))
            out[8] = (self.sel(swap, pl.ds(2, 2), st(g0, 1), ALL), self.sel(swap, pl.ds(2, 2), st(g0, 2), ALL), self.to(swap, dg=-1))
        else:
            sg = 1 if part == "C" else -1
            out[0] = (self.sel(swap, f0, g0, x), self.sel(swap, st(f0, -1), g0, x), self.to(swap, df=1))
            out[1] = (self.sel(swap, f0, g0, x), self.sel(swap, st(f0, 1), g0, x), self.to(swap, df=-1))
            out[2] = (self.sel(swap, st(f0, -sg), g0, x), self.sel(swap, st(f0, 2), g0, x), self.to(swap, df=sg))
            out[3] = (self.sel(swap, ALL, g0, x), self.sel(swap, ALL, st(g0, -1), x), self.to(swap, dg=1))
            out[4] = (self.sel(swap, ALL, g0, x), self.sel(swap, ALL, st(g0, 1), x), self.to(swap, dg=-1))
            out[5] = (self.sel(swap, pl.ds(0, 2), st(g0, -1), x), self.sel(swap, pl.ds(0, 2), st(g0, 2), x), self.to(swap, dg=1))
            out[6] = (self.sel(swap, pl.ds(2, 2), st(g0, 1), x), self.sel(swap, pl.ds(2, 2), st(g0, 2), x), self.to(swap, dg=-1))
            out[7] = (self.sel(swap, ALL, ALL, x), self.sel(swap, ALL, ALL, 1 - x), self.to(swap, dx=1))
        return out
    def plan(self):
        self.r = {p: self.ring(p in "BD", None, p) for p in "ABCD"}
    def start(self, s, part, *ks):
        if part in self.rows[s]:
            for k in ks:
                sent, _, to = self.r[part][k]
                self.copy(s, part, k, sent, to).start()
    def got(self, s, part, *ks):
        if part in self.rows[s]:
            for k in ks:
                _, came, to = self.r[part][k]
                self.copy(s, part, k, came, to).wait_recv()
    def sent(self, s):
        for part in self.rows[s]:
            for k in self.r[part]:
                sent, _, to = self.r[part][k]
                self.copy(s, part, k, sent, to).wait_send()
    def t0(self, s):
        for p in "CD": self.start(s, p, 0, 1)
        for p in "AB": self.start(s, p, 0)
    def t1(self, s):
        for p, k in (("C", 0), ("D", 1)):
            self.got(s, p, k); self.start(s, p, 2)
        for p in "AB":
            self.got(s, p, 0); self.start(s, p, 1, 2)
    def t2(self, s):
        for p, k in (("C", 1), ("D", 0)):
            self.got(s, p, k, 2); self.start(s, p, 3, 4)
        for p in "AB":
            self.got(s, p, 1); self.start(s, p, 3)
            self.got(s, p, 2); self.start(s, p, 4)
    def t3(self, s):
        for p in "CD":
            self.got(s, p, 3); self.start(s, p, 5)
            self.got(s, p, 4); self.start(s, p, 6)
        for p in "AB":
            self.got(s, p, 3, 4); self.start(s, p, 5, 6)
    def t4(self, s):
        for p in "CD":
            self.got(s, p, 5, 6); self.start(s, p, 7)
        for p in "AB":
            self.got(s, p, 5); self.start(s, p, 7)
            self.got(s, p, 6); self.start(s, p, 8)
    def t5(self, s):
        for p in "AB": self.got(s, p, 7, 8)
        for p in "CD": self.got(s, p, 7)
    def greet(self):
        barrier = pltpu.get_barrier_semaphore()
        for to in (self.dev(dz=1), self.dev(dz=-1), self.dev(dy=1), self.dev(dy=-1), self.dev(dx=1)):
            pl.semaphore_signal(barrier, inc=1, device_id=to, device_id_type=MESH)
        pl.semaphore_wait(barrier, 5)

QROWS = {"A": (0, 32), "B": (32, 32), "C": (64, 16), "D": (80, 16)}
OROWS = ({"A": (0, 32), "B": (32, 16), "C": (48, 16)}, {"A": (0, 16), "B": (16, 32), "D": (48, 16)})


def gather_kernel(wq, wo, gq, go, ssem, rsem, lsem):
    G = Gather(
        [gq.at[i] for i in range(4)] + [go.at[i] for i in range(2)],
        [QROWS] * 4 + list(OROWS),
        ssem,
        rsem,
    )
    G.plan()
    z, y, x = G.z, G.y, G.x
    own = [pltpu.make_async_copy(wq.at[i], gq.at[i, z, y, x], lsem.at[i]) for i in range(4)]
    own += [
        pltpu.make_async_copy(wo.at[:, pl.ds(768 * i, 768)], go.at[i, z, y, x], lsem.at[4 + i])
        for i in range(2)
    ]
    for c in own:
        c.start()
    G.greet()
    for c in own:
        c.wait()
    n = 6
    for t in (G.t0, G.t1, G.t2):
        for s in range(n):
            t(s)
    for s in range(n + 2):
        if s < n:
            G.t3(s)
        if 0 <= s - 1 < n:
            G.t4(s - 1)
        if 0 <= s - 2 < n:
            G.t5(s - 2)
    for s in range(n):
        G.sent(s)


def gathered(w_qkv, w_out):
    anywhere = pl.BlockSpec(memory_space=pl.ANY)
    wq = w_qkv.reshape(96, 4, 2, 3, 128).transpose(1, 0, 3, 2, 4).reshape(4, 96, 768)
    return pl.pallas_call(
        gather_kernel,
        in_specs=[anywhere] * 2,
        out_specs=(anywhere, anywhere),
        out_shape=(
            jax.ShapeDtypeStruct((4, 4, 4, 2, 96, 768), jnp.bfloat16),
            jax.ShapeDtypeStruct((2, 4, 4, 2, 64, 768), jnp.bfloat16),
        ),
        scratch_shapes=[
            pltpu.SemaphoreType.DMA((204,)),
            pltpu.SemaphoreType.DMA((204,)),
            pltpu.SemaphoreType.DMA((6,)),
        ],
        compiler_params=pltpu.CompilerParams(collective_id=0, has_side_effects=True),
        name="gather_weights",
    )(wq, w_out)


def passed_along(array, axis, by):
    size = lax.axis_size(axis)
    pairs = [(i, i + by) for i in range(size) if 0 <= i + by < size]
    return lax.ppermute(array, axis, pairs)


def qk_norm(values_in):
    return (values_in * lax.rsqrt(jnp.mean(jnp.square(values_in), -1, keepdims=True) + EPS)).astype(
        jnp.bfloat16
    )


def local(x_in, time_index, mod_table, w_qkv, w_out, stale_kv):
    n_segment = lax.axis_size("section")
    n_seq = lax.axis_size("seq")
    segment_id = lax.axis_index("section")
    images, patches, shard_rows, model_width = x_in.shape
    local_heads = w_qkv.shape[2]
    head_dim = w_qkv.shape[4]
    patch_len = shard_rows * n_seq
    col_width = model_width // n_seq
    steps_range = jnp.arange(mod_table.shape[1], dtype=jnp.int32)
    onehot = (time_index[:, None] == steps_range[None, :]).astype(jnp.float32)
    modulation = jnp.einsum("it,tcd->icd", onehot, mod_table[0], precision=lax.Precision.HIGHEST)
    shift_vec = modulation[None, :, 0]
    scale_vec = modulation[None, :, 1]
    gate_vec = modulation[None, :, 2]
    gq, go = gathered(w_qkv[0], w_out[0])
    proj_in = gq.reshape(4, model_width, 768).transpose(1, 0, 2).reshape(model_width, 3072)
    proj_out = go.reshape(2, 2048, 768).transpose(1, 0, 2).reshape(2048, 1536)
    start_table = stale_kv[0]
    inputs = jnp.transpose(x_in, (1, 2, 0, 3))

    def modulate(rows_in):
        rows_f32 = rows_in.astype(jnp.float32)
        row_mean = jnp.mean(rows_f32, -1, keepdims=True)
        row_var = jnp.mean(jnp.square(rows_f32 - row_mean), -1, keepdims=True)
        return (
            (rows_f32 - row_mean) * lax.rsqrt(row_var + EPS) * (1.0 + scale_vec) + shift_vec
        ).astype(jnp.bfloat16)

    def project(rows_mod):
        count = rows_mod.shape[0]
        qkv = jnp.dot(
            rows_mod.reshape(count * images, model_width),
            proj_in,
            preferred_element_type=jnp.float32,
        )
        qkv = qkv.reshape(count, images, 4, 3, 2, head_dim).transpose(0, 1, 2, 4, 3, 5)
        qkv = qkv.reshape(count, images, local_heads, 3, head_dim)
        return jnp.stack(
            (
                qk_norm(qkv[:, :, :, 0]),
                qk_norm(qkv[:, :, :, 1]),
                qkv[:, :, :, 2].astype(jnp.bfloat16),
            ),
            axis=3,
        )

    def no_project(rows_mod):
        return jnp.zeros((rows_mod.shape[0], images, local_heads, 3, head_dim), jnp.bfloat16)

    def attend(stacked, kv_table, patch_at):
        fresh_rows = jnp.transpose(stacked[:, :, :, 1:3], (1, 0, 3, 2, 4))
        kv_table = lax.dynamic_update_slice_in_dim(
            kv_table, fresh_rows, patch_at * patch_len, axis=1
        )
        queries = stacked[:, :, :, 0]
        scores = jnp.einsum(
            "qbhd,bkhd->bhqk", queries, kv_table[:, :, 0], preferred_element_type=jnp.float32
        ) / math.sqrt(head_dim)
        exp_scores = jnp.exp(scores)
        probs = (exp_scores / jnp.sum(exp_scores, -1, keepdims=True)).astype(jnp.bfloat16)
        mixed_heads = jnp.einsum(
            "bhqk,bkhd->qbhd", probs, kv_table[:, :, 1], preferred_element_type=jnp.float32
        )
        return (
            mixed_heads.astype(jnp.bfloat16).reshape(patch_len, images, local_heads * head_dim),
            kv_table,
        )

    def no_attend(stacked, kv_table, patch_at):
        return (jnp.zeros((patch_len, images, local_heads * head_dim), jnp.bfloat16), kv_table)

    def block_core(stacked, kv_table, patch_at, active):
        mixed_heads, kv_table = lax.cond(active, attend, no_attend, stacked, kv_table, patch_at)
        empty_cols = jnp.zeros((patch_len, images, col_width), jnp.float32)
        piece_rows = lax.all_gather(mixed_heads, "seq", axis=2, tiled=True)
        width_piece = piece_rows.shape[2]

        def added():
            term = jnp.dot(
                piece_rows.reshape(patch_len * images, width_piece),
                proj_out,
                preferred_element_type=jnp.float32,
            )
            return term.reshape(empty_cols.shape)

        attn_cols = lax.cond(active, added, lambda: empty_cols)
        return (attn_cols.astype(jnp.bfloat16), kv_table)

    out_start = jnp.zeros((patches, shard_rows, images, model_width), jnp.bfloat16)
    tick_count = n_segment + patches - 1

    def advance(tick, carry):
        incoming, kv_table, out_buf = carry
        patch_id = tick - segment_id
        active = jnp.logical_and(patch_id >= 0, patch_id < patches)
        patch_at = jnp.clip(patch_id, 0, patches - 1)
        first_rows = lax.dynamic_index_in_dim(inputs, patch_at, 0, keepdims=False)
        x_rows = jnp.where(segment_id == 0, first_rows, incoming)
        modulated = modulate(x_rows)
        stacked = lax.cond(
            active, project, no_project, lax.all_gather(modulated, "seq", axis=0, tiled=True)
        )
        attn_cols, kv_table = block_core(stacked, kv_table, patch_at, active)
        attn_rows = lax.all_to_all(attn_cols, "seq", split_axis=0, concat_axis=2, tiled=True)
        new_rows = (x_rows.astype(jnp.float32) + gate_vec * attn_rows.astype(jnp.float32)).astype(
            jnp.bfloat16
        )
        out_buf = jnp.where(
            active, lax.dynamic_update_index_in_dim(out_buf, new_rows, patch_at, 0), out_buf
        )
        incoming = passed_along(new_rows, "section", 1)
        return (incoming, kv_table, out_buf)

    carry_start = (
        jnp.zeros((shard_rows, images, model_width), jnp.bfloat16),
        start_table,
        out_start,
    )
    unused, end_table, out_buf = lax.fori_loop(0, tick_count, advance, carry_start)
    layer_out = jnp.transpose(out_buf, (2, 0, 1, 3))[None]
    fresh_kv = end_table[None]
    return (layer_out, fresh_kv)


def solution(mesh):
    placed = (
        P("dp", None, "seq", None),
        P("dp"),
        P("section", None, None, None),
        P("section", "dp", "seq", None, None),
        P("section", "dp", "seq"),
        P("section", "dp", None, None, "seq", None),
    )
    return jax.shard_map(
        local,
        mesh=mesh,
        in_specs=placed,
        out_specs=(
            P("section", "dp", None, "seq", None),
            P("section", "dp", None, None, "seq", None),
        ),
        check_vma=False,
    )
```

```python
import functools
import math

import jax
import jax.numpy as jnp
from jax import lax
from jax.experimental import pallas as pl
from jax.experimental.pallas import tpu as pltpu
from jax.sharding import PartitionSpec as P

EPS = 1e-06
MESH = pl.DeviceIdType.MESH
ALL = slice(None)
BF16 = jnp.bfloat16
F32 = jnp.float32
GROUP = 1

ROWS = {
    "q": {"A": (0, 32), "B": (32, 32), "C": (64, 16), "D": (80, 16)},
    "o0": {"A": (0, 32), "B": (32, 16), "C": (48, 16)},
    "o1": {"A": (0, 16), "B": (16, 32), "D": (48, 16)},
}
SEMS = 34
FIRST = {"q": 0, "o0": 4 * SEMS, "o1": 5 * SEMS}
PART = {"A": 0, "B": 9, "C": 18, "D": 26}


class Gather:
    def __init__(self, gq, go, ssem, rsem):
        dp = lax.axis_index("dp")
        self.z, self.y, self.x = lax.div(dp, 8), lax.rem(lax.div(dp, 2), 4), lax.rem(dp, 2)
        self.gq, self.go, self.ssem, self.rsem = gq, go, ssem, rsem
        self.r = {part: self.ring(part in "BD", part) for part in "ABCD"}

    def step(self, v, by):
        return lax.rem(v + (by + 4), 4)

    def dev(self, dz=0, dy=0, dx=0):
        z = self.step(self.z, dz) if dz else self.z
        y = self.step(self.y, dy) if dy else self.y
        x = 1 - self.x if dx else self.x
        return {"dp": z * 8 + y * 2 + x}

    def copy(self, stage, part, k, sel, to):
        kind, s = stage
        r0, n = ROWS[kind][part]
        rows = pl.ds(r0, n)
        if kind == "q":
            v = self.gq.at[(s, *sel, rows, ALL)]
        else:
            v = self.go.at[(s, *sel, rows, ALL)]
        i = FIRST[kind] + (s * SEMS if kind == "q" else 0) + PART[part] + k
        return pltpu.make_async_remote_copy(
            src_ref=v,
            dst_ref=v,
            send_sem=self.ssem.at[i],
            recv_sem=self.rsem.at[i],
            device_id=to,
            device_id_type=MESH,
        )

    def ring(self, swap, part):
        f0, g0 = (self.z, self.y) if swap else (self.y, self.z)
        st, x = self.step, self.x

        def sel(f, g, xs):
            return (f, g, xs) if swap else (g, f, xs)

        def to(df=0, dg=0, dx=0):
            return self.dev(dz=df, dy=dg, dx=dx) if swap else self.dev(dz=dg, dy=df, dx=dx)

        low, high = pl.ds(0, 2), pl.ds(2, 2)
        if part in "AB":
            return [
                (sel(f0, g0, x), sel(f0, g0, 1 - x), to(dx=1)),
                (sel(f0, g0, ALL), sel(st(f0, -1), g0, ALL), to(df=1)),
                (sel(f0, g0, ALL), sel(st(f0, 1), g0, ALL), to(df=-1)),
                (sel(st(f0, -1), g0, 0), sel(st(f0, 2), g0, 0), to(df=1)),
                (sel(st(f0, 1), g0, 1), sel(st(f0, 2), g0, 1), to(df=-1)),
                (sel(ALL, g0, ALL), sel(ALL, st(g0, -1), ALL), to(dg=1)),
                (sel(ALL, g0, ALL), sel(ALL, st(g0, 1), ALL), to(dg=-1)),
                (sel(low, st(g0, -1), ALL), sel(low, st(g0, 2), ALL), to(dg=1)),
                (sel(high, st(g0, 1), ALL), sel(high, st(g0, 2), ALL), to(dg=-1)),
            ]
        sg = 1 if part == "C" else -1
        return [
            (sel(f0, g0, x), sel(st(f0, -1), g0, x), to(df=1)),
            (sel(f0, g0, x), sel(st(f0, 1), g0, x), to(df=-1)),
            (sel(st(f0, -sg), g0, x), sel(st(f0, 2), g0, x), to(df=sg)),
            (sel(ALL, g0, x), sel(ALL, st(g0, -1), x), to(dg=1)),
            (sel(ALL, g0, x), sel(ALL, st(g0, 1), x), to(dg=-1)),
            (sel(low, st(g0, -1), x), sel(low, st(g0, 2), x), to(dg=1)),
            (sel(high, st(g0, 1), x), sel(high, st(g0, 2), x), to(dg=-1)),
            (sel(ALL, ALL, x), sel(ALL, ALL, 1 - x), to(dx=1)),
        ]

    def start(self, stage, part, *ks):
        if part in ROWS[stage[0]]:
            for k in ks:
                out, _, to = self.r[part][k]
                self.copy(stage, part, k, out, to).start()

    def got(self, stage, part, *ks):
        if part in ROWS[stage[0]]:
            for k in ks:
                _, came, to = self.r[part][k]
                self.copy(stage, part, k, came, to).wait_recv()

    def sent(self, stage):
        for part in ROWS[stage[0]]:
            for k, (out, _, to) in enumerate(self.r[part]):
                self.copy(stage, part, k, out, to).wait_send()

    def t0(self, s):
        for p in "CD":
            self.start(s, p, 0, 1)
        for p in "AB":
            self.start(s, p, 0)

    def t1(self, s):
        for p, k in (("C", 0), ("D", 1)):
            self.got(s, p, k)
            self.start(s, p, 2)
        for p in "AB":
            self.got(s, p, 0)
            self.start(s, p, 1, 2)

    def t2(self, s):
        for p, k in (("C", 1), ("D", 0)):
            self.got(s, p, k, 2)
            self.start(s, p, 3, 4)
        for p in "AB":
            self.got(s, p, 1)
            self.start(s, p, 3)
            self.got(s, p, 2)
            self.start(s, p, 4)

    def t3(self, s):
        for p in "CD":
            self.got(s, p, 3)
            self.start(s, p, 5)
            self.got(s, p, 4)
            self.start(s, p, 6)
        for p in "AB":
            self.got(s, p, 3, 4)
            self.start(s, p, 5, 6)

    def t4(self, s):
        for p in "CD":
            self.got(s, p, 5, 6)
            self.start(s, p, 7)
        for p in "AB":
            self.got(s, p, 5)
            self.start(s, p, 7)
            self.got(s, p, 6)
            self.start(s, p, 8)

    def t5(self, s):
        for p in "AB":
            self.got(s, p, 7, 8)
        for p in "CD":
            self.got(s, p, 7)


def kernel(
    x_ref,
    mod_ref,
    wq_ref,
    wo_ref,
    stale_ref,
    out_ref,
    kv_out_ref,
    gq,
    go,
    mod_rows,
    mixed,
    att,
    came,
    rows_out,
    kv,
    ssem,
    rsem,
    lsem,
    core_s,
    core_r,
    sec_s,
    sec_r,
    done_sem,
):
    sec, me = lax.axis_index("section"), lax.axis_index("seq")
    first = sec == 0
    other = {"seq": 1 - me}
    G = Gather(gq, go, ssem, rsem)
    own = [pltpu.make_async_copy(wq_ref.at[i], gq.at[i, G.z, G.y, G.x], lsem.at[i]) for i in range(4)]
    own += [
        pltpu.make_async_copy(
            wo_ref.at[:, pl.ds(768 * i, 768)], go.at[i, G.z, G.y, G.x], lsem.at[4 + i]
        )
        for i in range(2)
    ]
    table = pltpu.make_async_copy(stale_ref, kv, lsem.at[6])
    for c in own:
        c.start()
    table.start()
    barrier = pltpu.get_barrier_semaphore()
    for to in (
        G.dev(dz=1), G.dev(dz=-1), G.dev(dy=1), G.dev(dy=-1), G.dev(dx=1), other, {"section": 1 - sec},
    ):
        pl.semaphore_signal(barrier, inc=1, device_id=to, device_id_type=MESH)
    for c in own:
        c.wait()
    pl.semaphore_wait(barrier, 7)

    def to_core(v, i):
        return pltpu.make_async_remote_copy(
            src_ref=v, dst_ref=v, send_sem=core_s.at[i], recv_sem=core_r.at[i], device_id=other, device_id_type=MESH
        )

    def rows_copy(p, owner):
        return to_core(mod_rows.at[p, owner], p)

    def pair_copy(s, owner):
        return to_core(mixed.at[owner, :, :, pl.ds(pl.multiple_of(s * 256, 256), 256)], 4 + s)

    def mixed_copy(p, owner):
        return to_core(mixed.at[owner, p], 4 + p)

    def att_copy(j, p, owner):
        return to_core(att.at[owner, j, p, 1 - owner], 8 + 4 * j + p)

    def hand_over(j, p, cc):
        cols = pl.ds(cc * 1536 + j * 768, 768)
        i = 8 * j + 2 * p + cc
        return pltpu.make_async_remote_copy(
            src_ref=rows_out.at[p, :, cols],
            dst_ref=came.at[p, :, cols],
            send_sem=sec_s.at[i],
            recv_sem=sec_r.at[i],
            device_id={"section": 1 - sec},
            device_id_type=MESH,
        )

    def rows_done(p):
        return pltpu.make_async_copy(rows_out.at[p], out_ref.at[p], done_sem.at[p])

    def modulate(x, p):
        rows = x[p].astype(F32)
        mean = jnp.mean(rows, -1, keepdims=True)
        cent = rows - mean
        var = jnp.mean(jnp.square(cent), -1, keepdims=True)
        mod_rows[p, me] = (
            cent * lax.rsqrt(var + EPS) * (1.0 + mod_ref[1:2]) + mod_ref[0:1]
        ).astype(BF16)

    def normed(a):
        return (a * lax.rsqrt(jnp.mean(jnp.square(a), -1, keepdims=True) + EPS)).astype(BF16)

    def heads(s, p0, np_):
        n = np_ * 128
        m = mod_rows[p0 : p0 + np_].reshape(n, 3072)

        def part(t):
            w = gq[s, :, :, :, :, t * 256 : (t + 1) * 256].reshape(3072, 256)
            return jnp.dot(m, w, preferred_element_type=F32)

        q2, k2, v2 = part(0), part(1), part(2)
        for hh in range(2):
            h = 2 * s + hh
            cols = slice(hh * 128, (hh + 1) * 128)
            q, k, v = normed(q2[:, cols]), normed(k2[:, cols]), v2[:, cols].astype(BF16)
            for i in range(np_):
                p = p0 + i
                at = slice(p * 128, (p + 1) * 128)
                here = slice(i * 128, (i + 1) * 128)
                kv[h, 0, at] = k[here]
                kv[h, 1, at] = v[here]
                score = lax.dot_general(
                    q[here], kv[h, 0], (((1,), (1,)), ((), ())), preferred_element_type=F32
                )
                e = jnp.exp2(score * (math.log2(math.e) / math.sqrt(128.0)))
                total = jnp.sum(e, -1, keepdims=True)
                mix = jnp.dot(e.astype(BF16), kv[h, 1], preferred_element_type=F32)
                mixed[me, p, :, pl.ds(pl.multiple_of(h * 128, 128), 128)] = (mix / total).astype(BF16)

    def columns(j, p0, np_):
        n = np_ * 128
        total = None
        for cc in range(2):
            a = mixed[cc, p0 : p0 + np_].reshape(n, 1024)
            w = go[j, 2 * cc : 2 * cc + 2].reshape(1024, 768)
            term = jnp.dot(a, w, preferred_element_type=F32)
            total = term if total is None else total + term
        att[me, j, p0 : p0 + np_] = total.astype(BF16).reshape(np_, 2, 64, 768)
        for p in range(p0, p0 + np_):
            att_copy(j, p, me).start()

    def finish(x, j, p):
        att_copy(j, p, 1 - me).wait_recv()
        for cc in range(2):
            cols = slice(cc * 1536 + j * 768, cc * 1536 + (j + 1) * 768)
            rows_out[p, :, cols] = (
                x[p, :, cols].astype(F32) + mod_ref[2:3, cols] * att[cc, j, p, me].astype(F32)
            ).astype(BF16)

    q_stages = [("q", s) for s in range(4)]
    o_stages = [("o0", 0), ("o1", 1)]
    for s in q_stages + o_stages:
        G.t0(s)

    @pl.when(first)
    def _():
        for p in range(4):
            modulate(x_ref, p)
            rows_copy(p, me).start()

    for s in q_stages + o_stages:
        G.t1(s)
    for s in q_stages + o_stages:
        G.t2(s)
    G.t3(q_stages[0])
    G.t3(q_stages[1])
    table.wait()

    @pl.when(first)
    def _():
        for p in range(4):
            rows_copy(p, 1 - me).wait_recv()

    def advance(s, carry):
        G.t4(("q", s))

        @pl.when(s < 2)
        def _():
            G.t3(("q", s + 2))

        @pl.when(s == 2)
        def _():
            G.t3(o_stages[0])

        @pl.when(s == 3)
        def _():
            G.t3(o_stages[1])

        G.t5(("q", s))

        @pl.when(first)
        def _():
            heads(s, 0, 4)
            pair_copy(s, me).start()

        return carry

    lax.fori_loop(0, 4, advance, 0)
    G.t4(o_stages[0])
    G.t5(o_stages[0])

    @pl.when(first)
    def _():
        pltpu.make_async_copy(kv, kv_out_ref, done_sem.at[4]).start()
        for s in range(4):
            pair_copy(s, 1 - me).wait_recv()

    def first_half(j):
        for p0 in (0, 2):
            columns(j, p0, 2)
        for p in range(4):
            finish(x_ref, j, p)
            for cc in range(2):
                hand_over(j, p, cc).start()
            if j == 1:
                rows_done(p).start()

    @pl.when(first)
    def _():
        first_half(0)

    G.t4(o_stages[1])
    G.t5(o_stages[1])

    @pl.when(first)
    def _():
        first_half(1)

    @pl.when(jnp.logical_not(first))
    def _():
        for p0 in range(0, 4, GROUP):
            group = range(p0, p0 + GROUP)
            for p in group:
                for j in range(2):
                    for cc in range(2):
                        hand_over(j, p, cc).wait_recv()
                modulate(came, p)
                rows_copy(p, me).start()
            for p in group:
                rows_copy(p, 1 - me).wait_recv()

            def one(s, carry):
                heads(s, p0, GROUP)
                return carry

            lax.fori_loop(0, 4, one, 0)
            for p in group:
                mixed_copy(p, me).start()
            if p0 + GROUP == 4:
                pltpu.make_async_copy(kv, kv_out_ref, done_sem.at[4]).start()
            for p in group:
                mixed_copy(p, 1 - me).wait_recv()
            for j in range(2):
                columns(j, p0, GROUP)
            for p in group:
                for j in range(2):
                    finish(came, j, p)
                rows_done(p).start()

    for p in range(4):
        rows_done(p).wait()
    pltpu.make_async_copy(kv, kv_out_ref, done_sem.at[4]).wait()
    for s in q_stages + o_stages:
        G.sent(s)
    for p in range(4):
        rows_copy(p, me).wait_send()
        for j in range(2):
            att_copy(j, p, me).wait_send()

    @pl.when(first)
    def _():
        for p in range(4):
            pair_copy(p, me).wait_send()
            for j in range(2):
                for cc in range(2):
                    hand_over(j, p, cc).wait_send()

    @pl.when(jnp.logical_not(first))
    def _():
        for p in range(4):
            mixed_copy(p, me).wait_send()


def local(x_in, time_index, mod_table, w_qkv, w_out, stale_kv):
    modulation = lax.dynamic_index_in_dim(mod_table[0], time_index[0], 0, keepdims=False)
    wq = w_qkv[0].reshape(96, 4, 2, 3, 128).transpose(1, 0, 3, 2, 4).reshape(4, 96, 768)
    stale = stale_kv[0, 0].transpose(2, 1, 0, 3)
    anywhere = pl.BlockSpec(memory_space=pl.ANY)
    vmem = pl.BlockSpec(memory_space=pltpu.VMEM)
    dma = pltpu.SemaphoreType.DMA
    rows, kv = pl.pallas_call(
        kernel,
        in_specs=[vmem, vmem, anywhere, anywhere, anywhere],
        out_specs=(anywhere, anywhere),
        out_shape=(
            jax.ShapeDtypeStruct((4, 64, 3072), BF16),
            jax.ShapeDtypeStruct((8, 2, 512, 128), BF16),
        ),
        scratch_shapes=[
            pltpu.VMEM((4, 4, 4, 2, 96, 768), BF16),
            pltpu.VMEM((2, 4, 4, 2, 64, 768), BF16),
            pltpu.VMEM((4, 2, 64, 3072), BF16),
            pltpu.VMEM((2, 4, 128, 1024), BF16),
            pltpu.VMEM((2, 2, 4, 2, 64, 768), BF16),
            pltpu.VMEM((4, 64, 3072), BF16),
            pltpu.VMEM((4, 64, 3072), BF16),
            pltpu.VMEM((8, 2, 512, 128), BF16),
            dma((6 * SEMS,)),
            dma((6 * SEMS,)),
            dma((7,)),
            dma((16,)),
            dma((16,)),
            dma((16,)),
            dma((16,)),
            dma((5,)),
        ],
        compiler_params=pltpu.CompilerParams(
            collective_id=0, has_side_effects=True, vmem_limit_bytes=60 * 2**20
        ),
        cost_estimate=pl.CostEstimate(flops=14 * 10**9, bytes_accessed=10**7, transcendentals=2 * 10**6),
        name="two_blocks",
    )(x_in[0], modulation, wq, w_out[0], stale)
    return rows[None, None], kv.transpose(2, 1, 0, 3)[None, None]


def solution(mesh):
    placed = (
        P("dp", None, "seq", None),
        P("dp"),
        P("section", None, None, None),
        P("section", "dp", "seq", None, None),
        P("section", "dp", "seq"),
        P("section", "dp", None, None, "seq", None),
    )
    return jax.shard_map(
        local,
        mesh=mesh,
        in_specs=placed,
        out_specs=(
            P("section", "dp", None, "seq", None),
            P("section", "dp", None, None, "seq", None),
        ),
        check_vma=False,
    )
```

```python
import functools
import math

import jax
import jax.numpy as jnp
from jax import lax
from jax.experimental import pallas as pl
from jax.experimental.pallas import tpu as pltpu
from jax.sharding import PartitionSpec as P

EPS = 1e-06
MESH = pl.DeviceIdType.MESH
ALL = slice(None)
BF16 = jnp.bfloat16
F32 = jnp.float32

ROWS = {
    "q": {"A": (0, 32), "B": (32, 32), "C": (64, 16), "D": (80, 16)},
    "o0": {"A": (0, 32), "B": (32, 16), "C": (48, 16)},
    "o1": {"A": (0, 16), "B": (16, 32), "D": (48, 16)},
}
SEMS = 34
FIRST = {"q": 0, "o0": 4 * SEMS, "o1": 5 * SEMS}
PART = {"A": 0, "B": 9, "C": 18, "D": 26}


class Gather:
    def __init__(self, gq, go, ssem, rsem):
        dp = lax.axis_index("dp")
        self.z, self.y, self.x = lax.div(dp, 8), lax.rem(lax.div(dp, 2), 4), lax.rem(dp, 2)
        self.gq, self.go, self.ssem, self.rsem = gq, go, ssem, rsem
        self.r = {part: self.ring(part in "BD", part) for part in "ABCD"}

    def step(self, v, by):
        return lax.rem(v + (by + 4), 4)

    def dev(self, dz=0, dy=0, dx=0):
        z = self.step(self.z, dz) if dz else self.z
        y = self.step(self.y, dy) if dy else self.y
        x = 1 - self.x if dx else self.x
        return {"dp": z * 8 + y * 2 + x}

    def copy(self, stage, part, k, sel, to):
        kind, s = stage
        r0, n = ROWS[kind][part]
        rows = pl.ds(r0, n)
        if kind == "q":
            v = self.gq.at[(s, *sel, rows, ALL)]
        else:
            v = self.go.at[(s, *sel, rows, ALL)]
        i = FIRST[kind] + (s * SEMS if kind == "q" else 0) + PART[part] + k
        return pltpu.make_async_remote_copy(
            src_ref=v,
            dst_ref=v,
            send_sem=self.ssem.at[i],
            recv_sem=self.rsem.at[i],
            device_id=to,
            device_id_type=MESH,
        )

    def ring(self, swap, part):
        f0, g0 = (self.z, self.y) if swap else (self.y, self.z)
        st, x = self.step, self.x

        def sel(f, g, xs):
            return (f, g, xs) if swap else (g, f, xs)

        def to(df=0, dg=0, dx=0):
            return self.dev(dz=df, dy=dg, dx=dx) if swap else self.dev(dz=dg, dy=df, dx=dx)

        low, high = pl.ds(0, 2), pl.ds(2, 2)
        if part in "AB":
            return [
                (sel(f0, g0, x), sel(f0, g0, 1 - x), to(dx=1)),
                (sel(f0, g0, ALL), sel(st(f0, -1), g0, ALL), to(df=1)),
                (sel(f0, g0, ALL), sel(st(f0, 1), g0, ALL), to(df=-1)),
                (sel(st(f0, -1), g0, 0), sel(st(f0, 2), g0, 0), to(df=1)),
                (sel(st(f0, 1), g0, 1), sel(st(f0, 2), g0, 1), to(df=-1)),
                (sel(ALL, g0, ALL), sel(ALL, st(g0, -1), ALL), to(dg=1)),
                (sel(ALL, g0, ALL), sel(ALL, st(g0, 1), ALL), to(dg=-1)),
                (sel(low, st(g0, -1), ALL), sel(low, st(g0, 2), ALL), to(dg=1)),
                (sel(high, st(g0, 1), ALL), sel(high, st(g0, 2), ALL), to(dg=-1)),
            ]
        sg = 1 if part == "C" else -1
        return [
            (sel(f0, g0, x), sel(st(f0, -1), g0, x), to(df=1)),
            (sel(f0, g0, x), sel(st(f0, 1), g0, x), to(df=-1)),
            (sel(st(f0, -sg), g0, x), sel(st(f0, 2), g0, x), to(df=sg)),
            (sel(ALL, g0, x), sel(ALL, st(g0, -1), x), to(dg=1)),
            (sel(ALL, g0, x), sel(ALL, st(g0, 1), x), to(dg=-1)),
            (sel(low, st(g0, -1), x), sel(low, st(g0, 2), x), to(dg=1)),
            (sel(high, st(g0, 1), x), sel(high, st(g0, 2), x), to(dg=-1)),
            (sel(ALL, ALL, x), sel(ALL, ALL, 1 - x), to(dx=1)),
        ]

    def start(self, stage, part, *ks):
        if part in ROWS[stage[0]]:
            for k in ks:
                out, _, to = self.r[part][k]
                self.copy(stage, part, k, out, to).start()

    def got(self, stage, part, *ks):
        if part in ROWS[stage[0]]:
            for k in ks:
                _, came, to = self.r[part][k]
                self.copy(stage, part, k, came, to).wait_recv()

    def sent(self, stage):
        for part in ROWS[stage[0]]:
            for k, (out, _, to) in enumerate(self.r[part]):
                self.copy(stage, part, k, out, to).wait_send()

    def t0(self, s):
        for p in "CD":
            self.start(s, p, 0, 1)
        for p in "AB":
            self.start(s, p, 0)

    def cd1(self, s):
        for p, k in (("C", 0), ("D", 1)):
            self.got(s, p, k)
            self.start(s, p, 2)

    def ab1(self, s):
        for p in "AB":
            self.got(s, p, 0)
            self.start(s, p, 1, 2)

    def cd2(self, s):
        for p, k in (("C", 1), ("D", 0)):
            self.got(s, p, k, 2)
            self.start(s, p, 3, 4)

    def ab2(self, s):
        for p in "AB":
            self.got(s, p, 1)
            self.start(s, p, 3)
            self.got(s, p, 2)
            self.start(s, p, 4)

    def cd3(self, s):
        for p in "CD":
            self.got(s, p, 3)
            self.start(s, p, 5)
            self.got(s, p, 4)
            self.start(s, p, 6)

    def ab3(self, s):
        for p in "AB":
            self.got(s, p, 3, 4)
            self.start(s, p, 5, 6)

    def cd4(self, s):
        for p in "CD":
            self.got(s, p, 5, 6)
            self.start(s, p, 7)

    def ab4(self, s):
        for p in "AB":
            self.got(s, p, 5)
            self.start(s, p, 7)
            self.got(s, p, 6)
            self.start(s, p, 8)

    def t5(self, s):
        for p in "AB":
            self.got(s, p, 7, 8)
        for p in "CD":
            self.got(s, p, 7)

    def tick(self, i, stages):
        for step, lag in (
            (self.cd1, 0),
            (self.cd2, 1),
            (self.t0, -2),
            (self.ab1, 0),
            (self.ab2, 1),
            (self.ab3, 2),
            (self.cd3, 1),
            (self.cd4, 2),
            (self.ab4, 3),
            (self.t5, 4),
        ):
            if 0 <= i - lag < len(stages):
                step(stages[i - lag])


class HalfGather(Gather):
    SPLIT = {"q": 48, "o": 32}

    def __init__(self, wq, wo, *rest):
        super().__init__(*rest)
        self.wq, self.wo = wq, wo

    def copy(self, stage, part, k, sel, to):
        kind, s = stage
        n = self.SPLIT[kind]
        i = ((0 if kind == "q" else 2) + s) * 18 + PART[part] + k
        rows = pl.ds(0 if part == "A" else n, n)
        buf = self.gq if kind == "q" else self.go
        if k == 0:
            v = buf.at[(s, *sel, ALL, ALL)]
            src = self.wq.at[2 * (1 - self.x) + s] if kind == "q" else self.wo.at[:, pl.ds(768 * s, 768)]
        else:
            v = src = buf.at[(s, *sel, rows, ALL)]
        return pltpu.make_async_remote_copy(
            src_ref=src,
            dst_ref=v,
            send_sem=self.ssem.at[i],
            recv_sem=self.rsem.at[i],
            device_id=to,
            device_id_type=MESH,
        )

    def start(self, stage, part, *ks):
        for k in ks:
            out, _, to = self.r[part][k]
            self.copy(stage, part, k, out, to).start()

    def got(self, stage, part, *ks):
        for k in ks:
            _, came, to = self.r[part][k]
            self.copy(stage, part, k, came, to).wait_recv()

    def sent(self, stage):
        for part in "AB":
            for k in range(0 if part == "A" else 1, 9):
                out, _, to = self.r[part][k]
                self.copy(stage, part, k, out, to).wait_send()

    def t0(self, s):
        self.start(s, "A", 0)

    def t1(self, s):
        self.got(s, "A", 0)
        for p in "AB":
            self.start(s, p, 1, 2)

    t2, t3, t4 = Gather.ab2, Gather.ab3, Gather.ab4

    def t5(self, s):
        for p in "AB":
            self.got(s, p, 7, 8)


def kernel(
    x_ref,
    mod_ref,
    wq_ref,
    wo_ref,
    stale_ref,
    out_ref,
    kv_out_ref,
    gq,
    go,
    mod_rows,
    mixed,
    att,
    came,
    rows_out,
    kv,
    mod_other,
    qkv_out,
    qkv_in,
    ssem,
    rsem,
    lsem,
    core_s,
    core_r,
    sec_s,
    sec_r,
    x_s,
    x_r,
    done_sem,
):
    sec, me = lax.axis_index("section"), lax.axis_index("seq")
    first = sec == 0
    other = {"seq": 1 - me}
    G = Gather(gq, go, ssem, rsem)
    H = HalfGather(wq_ref, wo_ref, gq, go, ssem, rsem)
    own_q = [pltpu.make_async_copy(wq_ref.at[i], gq.at[i, G.z, G.y, G.x], lsem.at[i]) for i in range(4)]
    half_q = [
        pltpu.make_async_copy(wq_ref.at[2 * G.x + i], gq.at[i, G.z, G.y, G.x], lsem.at[i])
        for i in range(2)
    ]
    own_o = [
        pltpu.make_async_copy(
            wo_ref.at[:, pl.ds(768 * i, 768)], go.at[i, G.z, G.y, G.x], lsem.at[4 + i]
        )
        for i in range(2)
    ]
    table = pltpu.make_async_copy(stale_ref, kv, lsem.at[6])
    for c in own_o:
        c.start()
    table.start()
    barrier = pltpu.get_barrier_semaphore()
    for to in (
        G.dev(dz=1), G.dev(dz=-1), G.dev(dy=1), G.dev(dy=-1), G.dev(dx=1), other, {"section": 1 - sec},
    ):
        pl.semaphore_signal(barrier, inc=1, device_id=to, device_id_type=MESH)
    pl.semaphore_wait(barrier, 7)

    def to_core(v, i):
        return pltpu.make_async_remote_copy(
            src_ref=v, dst_ref=v, send_sem=core_s.at[i], recv_sem=core_r.at[i], device_id=other, device_id_type=MESH
        )

    def rows_copy(p, owner):
        return to_core(mod_rows.at[p, owner], p)

    def other_copy(p, owner):
        return to_core(mod_other.at[p, owner], 16 + p)

    def to_chip(src, dst, i):
        return pltpu.make_async_remote_copy(
            src_ref=src, dst_ref=dst, send_sem=x_s.at[i], recv_sem=x_r.at[i], device_id=G.dev(dx=1), device_id_type=MESH
        )

    def lend(p):
        return to_chip(mod_rows.at[p, me], mod_other.at[p, me], p)

    def give_back(s, p):
        return to_chip(qkv_out.at[s, p], qkv_in.at[s, p], 4 + 4 * s + p)

    def mixed_copy(p, owner):
        return to_core(mixed.at[owner, p], 4 + p)

    def att_copy(j, p, owner):
        return to_core(att.at[owner, j, p, 1 - owner], 8 + 4 * j + p)

    def hand_over(j, p, cc):
        cols = pl.ds(cc * 1536 + j * 768, 768)
        i = 8 * j + 2 * p + cc
        return pltpu.make_async_remote_copy(
            src_ref=rows_out.at[p, :, cols],
            dst_ref=came.at[p, :, cols],
            send_sem=sec_s.at[i],
            recv_sem=sec_r.at[i],
            device_id={"section": 1 - sec},
            device_id_type=MESH,
        )

    def rows_done(p):
        return pltpu.make_async_copy(rows_out.at[p], out_ref.at[p], done_sem.at[p])

    def modulate(x, p):
        rows = x[p].astype(F32)
        mean = jnp.mean(rows, -1, keepdims=True)
        cent = rows - mean
        var = jnp.mean(jnp.square(cent), -1, keepdims=True)
        mod_rows[p, me] = (
            cent * lax.rsqrt(var + EPS) * (1.0 + mod_ref[1:2]) + mod_ref[0:1]
        ).astype(BF16)

    def normed(a):
        return (a * lax.rsqrt(jnp.mean(jnp.square(a), -1, keepdims=True) + EPS)).astype(BF16)

    def qkv(s, m):
        def part(t):
            w = gq[s, :, :, :, :, t * 256 : (t + 1) * 256].reshape(3072, 256)
            return jnp.dot(m, w, preferred_element_type=F32)

        return part(0), part(1), part(2)

    def attend(h, p, q, k, v):
        at = slice(p * 128, (p + 1) * 128)
        kv[h, 0, at] = k
        kv[h, 1, at] = v
        score = lax.dot_general(q, kv[h, 0], (((1,), (1,)), ((), ())), preferred_element_type=F32)
        e = jnp.exp2(score * (math.log2(math.e) / math.sqrt(128.0)))
        total = jnp.sum(e, -1, keepdims=True)
        mix = jnp.dot(e.astype(BF16), kv[h, 1], preferred_element_type=F32)
        mixed[me, p, :, pl.ds(pl.multiple_of(h * 128, 128), 128)] = (mix / total).astype(BF16)

    def heads(s, pair, p0, np_):
        m = mod_rows[p0 : p0 + np_].reshape(np_ * 128, 3072)
        q2, k2, v2 = qkv(s, m)
        for hh in range(2):
            cols = slice(hh * 128, (hh + 1) * 128)
            q, k, v = normed(q2[:, cols]), normed(k2[:, cols]), v2[:, cols].astype(BF16)
            for i in range(np_):
                here = slice(i * 128, (i + 1) * 128)
                attend(2 * pair + hh, p0 + i, q[here], k[here], v[here])

    def qkv_other(s):
        q2, k2, v2 = qkv(s, mod_other[...].reshape(512, 3072))
        for hh in range(2):
            cols = slice(hh * 128, (hh + 1) * 128)
            parts = (normed(q2[:, cols]), normed(k2[:, cols]), v2[:, cols].astype(BF16))
            for t, part in enumerate(parts):
                qkv_out[s, :, :, t * 256 + hh * 128 : t * 256 + (hh + 1) * 128] = part.reshape(4, 128, 128)
        for p in range(4):
            give_back(s, p).start()

    def attend_back(s, p):
        give_back(s, p).wait_recv()
        for hh in range(2):
            q, k, v = (
                qkv_in[s, p, :, t * 256 + hh * 128 : t * 256 + (hh + 1) * 128] for t in range(3)
            )
            attend(2 * (2 * (1 - G.x) + s) + hh, p, q, k, v)

    def columns(j, p0, np_):
        n = np_ * 128
        total = None
        for cc in range(2):
            a = mixed[cc, p0 : p0 + np_].reshape(n, 1024)
            w = go[j, 2 * cc : 2 * cc + 2].reshape(1024, 768)
            term = jnp.dot(a, w, preferred_element_type=F32)
            total = term if total is None else total + term
        att[me, j, p0 : p0 + np_] = total.astype(BF16).reshape(np_, 2, 64, 768)
        for p in range(p0, p0 + np_):
            att_copy(j, p, me).start()

    def finish(x, j, p):
        att_copy(j, p, 1 - me).wait_recv()
        for cc in range(2):
            cols = slice(cc * 1536 + j * 768, cc * 1536 + (j + 1) * 768)
            rows_out[p, :, cols] = (
                x[p, :, cols].astype(F32) + mod_ref[2:3, cols] * att[cc, j, p, me].astype(F32)
            ).astype(BF16)

    stages = [("q", s) for s in range(4)] + [("o0", 0), ("o1", 1)]
    halves = [("q", 0), ("q", 1), ("o", 0), ("o", 1)]
    table_out = pltpu.make_async_copy(kv, kv_out_ref, done_sem.at[4])

    @pl.when(first)
    def _():
        q0, q1, o0, o1 = halves

        def lent(p):
            lend(p).wait_recv()
            other_copy(p, me).start()

        H.t0(q0)
        for c in half_q:
            c.start()
        H.t0(q1)
        H.t0(o0)
        for p in range(2):
            modulate(x_ref, p)
            lend(p).start()
            rows_copy(p, me).start()
        for c in half_q + own_o:
            c.wait()
        H.t1(q0)
        for p in range(2, 4):
            modulate(x_ref, p)
            rows_copy(p, me).start()
        H.t2(q0)
        H.t1(q1)
        H.t3(q0)
        H.t2(q1)
        lent(0)
        lend(2).start()
        H.t4(q0)
        H.t3(q1)
        lent(1)
        lend(3).start()
        H.t5(q0)
        H.t1(o0)
        H.t0(o1)
        lent(2)
        table.wait()
        for p in range(4):
            rows_copy(p, 1 - me).wait_recv()
        lent(3)
        for p in range(4):
            other_copy(p, 1 - me).wait_recv()
        qkv_other(0)
        H.t1(o1)
        H.t2(o0)
        H.t4(q1)
        H.t2(o1)
        heads(0, 2 * G.x, 0, 4)
        H.t3(o0)
        H.t5(q1)
        H.t3(o1)
        qkv_other(1)
        H.t4(o0)
        heads(1, 2 * G.x + 1, 0, 4)
        H.t4(o1)
        for p in range(4):
            attend_back(0, p)

        def hand(j, p):
            finish(x_ref, j, p)
            u = 4 * j + p
            for cc in range(2):
                if u >= 2:
                    hand_over((u - 2) // 4, (u - 2) % 4, cc).wait_send()
                hand_over(j, p, cc).start()
            if j == 1:
                rows_done(p).start()

        for p in range(6):
            if p < 4:
                attend_back(1, p)
                mixed_copy(p, me).start()
            if p == 3:
                table_out.start()
            if 0 <= p - 1 < 4:
                if p == 1:
                    H.t5(o0)
                mixed_copy(p - 1, 1 - me).wait_recv()
                columns(0, p - 1, 1)
            if 0 <= p - 2 < 4:
                hand(0, p - 2)
        H.t5(o1)
        for p in range(5):
            if p < 4:
                columns(1, p, 1)
            if p > 0:
                hand(1, p - 1)

    @pl.when(jnp.logical_not(first))
    def _():
        for c in own_q:
            c.start()
        for c in own_q + own_o:
            c.wait()
        G.t0(stages[0])
        G.t0(stages[1])
        for i in range(9):
            G.tick(i, stages)
        table.wait()

        def rows_in(p):
            for j in range(2):
                for cc in range(2):
                    hand_over(j, p, cc).wait_recv()
            modulate(came, p)
            rows_copy(p, me).start()

        def all_columns(p):
            mixed_copy(p, 1 - me).wait_recv()
            for j in range(2):
                columns(j, p, 1)

        def all_finish(p):
            for j in range(2):
                finish(came, j, p)
            rows_done(p).start()

        for p in range(4):
            rows_in(p)
            if p == 1:
                G.tick(9, stages)
            if p > 0:
                all_columns(p - 1)
            rows_copy(p, 1 - me).wait_recv()

            def one(s, carry):
                heads(s, s, p, 1)
                return carry

            lax.fori_loop(0, 4, one, 0)
            mixed_copy(p, me).start()
            if p > 0:
                all_finish(p - 1)
        table_out.start()
        all_columns(3)
        all_finish(3)

    for p in range(4):
        rows_done(p).wait()
        rows_copy(p, me).wait_send()
        for j in range(2):
            att_copy(j, p, me).wait_send()
    table_out.wait()

    @pl.when(first)
    def _():
        for s in halves:
            H.sent(s)
        for p in range(4):
            lend(p).wait_send()
            other_copy(p, me).wait_send()
            mixed_copy(p, me).wait_send()
            for j in range(2):
                give_back(j, p).wait_send()
        for p in (2, 3):
            for cc in range(2):
                hand_over(1, p, cc).wait_send()

    @pl.when(jnp.logical_not(first))
    def _():
        for s in stages:
            G.sent(s)
        for p in range(4):
            mixed_copy(p, me).wait_send()


def local(x_in, time_index, mod_table, w_qkv, w_out, stale_kv):
    modulation = lax.dynamic_index_in_dim(mod_table[0], time_index[0], 0, keepdims=False)
    wq = w_qkv[0].reshape(96, 4, 2, 3, 128).transpose(1, 0, 3, 2, 4).reshape(4, 96, 768)
    stale = stale_kv[0, 0].transpose(2, 1, 0, 3)
    anywhere = pl.BlockSpec(memory_space=pl.ANY)
    vmem = pl.BlockSpec(memory_space=pltpu.VMEM)
    dma = pltpu.SemaphoreType.DMA
    rows, kv = pl.pallas_call(
        kernel,
        in_specs=[vmem, vmem, anywhere, anywhere, anywhere],
        out_specs=(anywhere, anywhere),
        out_shape=(
            jax.ShapeDtypeStruct((4, 64, 3072), BF16),
            jax.ShapeDtypeStruct((8, 2, 512, 128), BF16),
        ),
        scratch_shapes=[
            pltpu.VMEM((4, 4, 4, 2, 96, 768), BF16),
            pltpu.VMEM((2, 4, 4, 2, 64, 768), BF16),
            pltpu.VMEM((4, 2, 64, 3072), BF16),
            pltpu.VMEM((2, 4, 128, 1024), BF16),
            pltpu.VMEM((2, 2, 4, 2, 64, 768), BF16),
            pltpu.VMEM((4, 64, 3072), BF16),
            pltpu.VMEM((4, 64, 3072), BF16),
            pltpu.VMEM((8, 2, 512, 128), BF16),
            pltpu.VMEM((4, 2, 64, 3072), BF16),
            pltpu.VMEM((2, 4, 128, 768), BF16),
            pltpu.VMEM((2, 4, 128, 768), BF16),
            dma((6 * SEMS,)),
            dma((6 * SEMS,)),
            dma((7,)),
            dma((20,)),
            dma((20,)),
            dma((16,)),
            dma((16,)),
            dma((12,)),
            dma((12,)),
            dma((5,)),
        ],
        compiler_params=pltpu.CompilerParams(
            collective_id=0, has_side_effects=True, vmem_limit_bytes=60 * 2**20
        ),
        cost_estimate=pl.CostEstimate(flops=14 * 10**9, bytes_accessed=10**7, transcendentals=2 * 10**6),
        name="two_blocks",
    )(x_in[0], modulation, wq, w_out[0], stale)
    return rows[None, None], kv.transpose(2, 1, 0, 3)[None, None]


def solution(mesh):
    placed = (
        P("dp", None, "seq", None),
        P("dp"),
        P("section", None, None, None),
        P("section", "dp", "seq", None, None),
        P("section", "dp", "seq"),
        P("section", "dp", None, None, "seq", None),
    )
    return jax.shard_map(
        local,
        mesh=mesh,
        in_specs=placed,
        out_specs=(
            P("section", "dp", None, "seq", None),
            P("section", "dp", None, None, "seq", None),
        ),
        check_vma=False,
    )
```

```python
import functools
import math

import jax
import jax.numpy as jnp
from jax import lax
from jax.experimental import pallas as pl
from jax.experimental.pallas import tpu as pltpu
from jax.sharding import PartitionSpec as P

EPS = 1e-06
PIECES = ((0, 0), (0, 1), (1, 0), (1, 1), (0, 2), (1, 2), (0, 3), (1, 3))
MESH = pl.DeviceIdType.MESH
ALL = slice(None)
BF16 = jnp.bfloat16
F32 = jnp.float32

ROWS = {
    "q": {"A": (0, 32), "B": (32, 32), "C": (64, 16), "D": (80, 16)},
    "o0": {"A": (0, 32), "B": (32, 16), "C": (48, 16)},
    "o1": {"A": (0, 16), "B": (16, 32), "D": (48, 16)},
}
SEMS = 34
FIRST = {"q": 0, "o0": 4 * SEMS, "o1": 5 * SEMS}
PART = {"A": 0, "B": 9, "C": 18, "D": 26}


class Gather:
    def __init__(self, gq, go, ssem, rsem):
        dp = lax.axis_index("dp")
        self.z, self.y, self.x = lax.div(dp, 8), lax.rem(lax.div(dp, 2), 4), lax.rem(dp, 2)
        self.gq, self.go, self.ssem, self.rsem = gq, go, ssem, rsem
        self.r = {part: self.ring(part in "BD", part) for part in "ABCD"}

    def step(self, v, by):
        return lax.rem(v + (by + 4), 4)

    def dev(self, dz=0, dy=0, dx=0):
        z = self.step(self.z, dz) if dz else self.z
        y = self.step(self.y, dy) if dy else self.y
        x = 1 - self.x if dx else self.x
        return {"dp": z * 8 + y * 2 + x}

    def copy(self, stage, part, k, sel, to):
        kind, s = stage
        r0, n = ROWS[kind][part]
        rows = pl.ds(r0, n)
        if kind == "q":
            v = self.gq.at[(s, *sel, rows, ALL)]
        else:
            v = self.go.at[(s, *sel, rows, ALL)]
        i = FIRST[kind] + (s * SEMS if kind == "q" else 0) + PART[part] + k
        return pltpu.make_async_remote_copy(
            src_ref=v,
            dst_ref=v,
            send_sem=self.ssem.at[i],
            recv_sem=self.rsem.at[i],
            device_id=to,
            device_id_type=MESH,
        )

    def ring(self, swap, part):
        f0, g0 = (self.z, self.y) if swap else (self.y, self.z)
        st, x = self.step, self.x

        def sel(f, g, xs):
            return (f, g, xs) if swap else (g, f, xs)

        def to(df=0, dg=0, dx=0):
            return self.dev(dz=df, dy=dg, dx=dx) if swap else self.dev(dz=dg, dy=df, dx=dx)

        low, high = pl.ds(0, 2), pl.ds(2, 2)
        if part in "AB":
            return [
                (sel(f0, g0, x), sel(f0, g0, 1 - x), to(dx=1)),
                (sel(f0, g0, ALL), sel(st(f0, -1), g0, ALL), to(df=1)),
                (sel(f0, g0, ALL), sel(st(f0, 1), g0, ALL), to(df=-1)),
                (sel(st(f0, -1), g0, 0), sel(st(f0, 2), g0, 0), to(df=1)),
                (sel(st(f0, 1), g0, 1), sel(st(f0, 2), g0, 1), to(df=-1)),
                (sel(ALL, g0, ALL), sel(ALL, st(g0, -1), ALL), to(dg=1)),
                (sel(ALL, g0, ALL), sel(ALL, st(g0, 1), ALL), to(dg=-1)),
                (sel(low, st(g0, -1), ALL), sel(low, st(g0, 2), ALL), to(dg=1)),
                (sel(high, st(g0, 1), ALL), sel(high, st(g0, 2), ALL), to(dg=-1)),
            ]
        sg = 1 if part == "C" else -1
        return [
            (sel(f0, g0, x), sel(st(f0, -1), g0, x), to(df=1)),
            (sel(f0, g0, x), sel(st(f0, 1), g0, x), to(df=-1)),
            (sel(st(f0, -sg), g0, x), sel(st(f0, 2), g0, x), to(df=sg)),
            (sel(ALL, g0, x), sel(ALL, st(g0, -1), x), to(dg=1)),
            (sel(ALL, g0, x), sel(ALL, st(g0, 1), x), to(dg=-1)),
            (sel(low, st(g0, -1), x), sel(low, st(g0, 2), x), to(dg=1)),
            (sel(high, st(g0, 1), x), sel(high, st(g0, 2), x), to(dg=-1)),
            (sel(ALL, ALL, x), sel(ALL, ALL, 1 - x), to(dx=1)),
        ]

    def start(self, stage, part, *ks):
        if part in ROWS[stage[0]]:
            for k in ks:
                out, _, to = self.r[part][k]
                self.copy(stage, part, k, out, to).start()

    def got(self, stage, part, *ks):
        if part in ROWS[stage[0]]:
            for k in ks:
                _, came, to = self.r[part][k]
                self.copy(stage, part, k, came, to).wait_recv()

    def sent(self, stage):
        for part in ROWS[stage[0]]:
            for k, (out, _, to) in enumerate(self.r[part]):
                self.copy(stage, part, k, out, to).wait_send()

    def t0(self, s):
        for p in "CD":
            self.start(s, p, 0, 1)
        for p in "AB":
            self.start(s, p, 0)

    def cd1(self, s):
        for p, k in (("C", 0), ("D", 1)):
            self.got(s, p, k)
            self.start(s, p, 2)

    def ab1(self, s):
        for p in "AB":
            self.got(s, p, 0)
            self.start(s, p, 1, 2)

    def cd2(self, s):
        for p, k in (("C", 1), ("D", 0)):
            self.got(s, p, k, 2)
            self.start(s, p, 3, 4)

    def ab2(self, s):
        for p in "AB":
            self.got(s, p, 1)
            self.start(s, p, 3)
            self.got(s, p, 2)
            self.start(s, p, 4)

    def cd3(self, s):
        for p in "CD":
            self.got(s, p, 3)
            self.start(s, p, 5)
            self.got(s, p, 4)
            self.start(s, p, 6)

    def ab3(self, s):
        for p in "AB":
            self.got(s, p, 3, 4)
            self.start(s, p, 5, 6)

    def cd4(self, s):
        for p in "CD":
            self.got(s, p, 5, 6)
            self.start(s, p, 7)

    def ab4(self, s):
        for p in "AB":
            self.got(s, p, 5)
            self.start(s, p, 7)
            self.got(s, p, 6)
            self.start(s, p, 8)

    def t5(self, s):
        for p in "AB":
            self.got(s, p, 7, 8)
        for p in "CD":
            self.got(s, p, 7)

    def tick(self, i, stages):
        for step, lag in (
            (self.cd1, 0),
            (self.cd2, 1),
            (self.t0, -2),
            (self.ab1, 0),
            (self.ab2, 1),
            (self.ab3, 2),
            (self.cd3, 1),
            (self.cd4, 2),
            (self.ab4, 3),
            (self.t5, 4),
        ):
            if 0 <= i - lag < len(stages):
                step(stages[i - lag])


class HalfGather(Gather):
    SPLIT = {"q": 48, "o": 32}

    def __init__(self, wq, wo, *rest):
        super().__init__(*rest)
        self.wq, self.wo = wq, wo

    def copy(self, stage, part, k, sel, to):
        kind, s = stage
        n = self.SPLIT[kind]
        i = ((0 if kind == "q" else 2) + s) * 18 + PART[part] + k
        rows = pl.ds(0 if part == "A" else n, n)
        buf = self.gq if kind == "q" else self.go
        if k == 0:
            v = buf.at[(s, *sel, ALL, ALL)]
            src = self.wq.at[2 * (1 - self.x) + s] if kind == "q" else self.wo.at[:, pl.ds(768 * s, 768)]
        else:
            v = src = buf.at[(s, *sel, rows, ALL)]
        return pltpu.make_async_remote_copy(
            src_ref=src,
            dst_ref=v,
            send_sem=self.ssem.at[i],
            recv_sem=self.rsem.at[i],
            device_id=to,
            device_id_type=MESH,
        )

    def start(self, stage, part, *ks):
        for k in ks:
            out, _, to = self.r[part][k]
            self.copy(stage, part, k, out, to).start()

    def got(self, stage, part, *ks):
        for k in ks:
            _, came, to = self.r[part][k]
            self.copy(stage, part, k, came, to).wait_recv()

    def sent(self, stage):
        for part in "AB":
            for k in range(0 if part == "A" else 1, 9):
                out, _, to = self.r[part][k]
                self.copy(stage, part, k, out, to).wait_send()

    def t0(self, s):
        self.start(s, "A", 0)

    def t1(self, s):
        self.got(s, "A", 0)
        for p in "AB":
            self.start(s, p, 1, 2)

    t2, t3, t4 = Gather.ab2, Gather.ab3, Gather.ab4

    def t5(self, s):
        for p in "AB":
            self.got(s, p, 7, 8)


def kernel(
    x_ref,
    mod_ref,
    wq_ref,
    wo_ref,
    stale_ref,
    out_ref,
    kv_out_ref,
    gq,
    go,
    mod_rows,
    mixed,
    att,
    came,
    rows_out,
    kv,
    mod_other,
    qkv_out,
    qkv_in,
    raw,
    keys,
    ssem,
    rsem,
    lsem,
    core_s,
    core_r,
    sec_s,
    sec_r,
    x_s,
    x_r,
    done_sem,
):
    sec, me = lax.axis_index("section"), lax.axis_index("seq")
    first = sec == 0
    other = {"seq": 1 - me}
    G = Gather(gq, go, ssem, rsem)
    H = HalfGather(wq_ref, wo_ref, gq, go, ssem, rsem)
    own_q = [pltpu.make_async_copy(wq_ref.at[i], gq.at[i, G.z, G.y, G.x], lsem.at[i]) for i in range(4)]
    half_q = [
        pltpu.make_async_copy(wq_ref.at[2 * G.x + i], gq.at[i, G.z, G.y, G.x], lsem.at[i])
        for i in range(2)
    ]
    own_o = [
        pltpu.make_async_copy(
            wo_ref.at[:, pl.ds(768 * i, 768)], go.at[i, G.z, G.y, G.x], lsem.at[4 + i]
        )
        for i in range(2)
    ]
    table = pltpu.make_async_copy(stale_ref, raw, lsem.at[6])
    for c in own_o:
        c.start()
    table.start()
    barrier = pltpu.get_barrier_semaphore()
    for to in (
        G.dev(dz=1), G.dev(dz=-1), G.dev(dy=1), G.dev(dy=-1), G.dev(dx=1), other, {"section": 1 - sec},
    ):
        pl.semaphore_signal(barrier, inc=1, device_id=to, device_id_type=MESH)
    pl.semaphore_wait(barrier, 7)

    def to_core(v, i):
        return pltpu.make_async_remote_copy(
            src_ref=v, dst_ref=v, send_sem=core_s.at[i], recv_sem=core_r.at[i], device_id=other, device_id_type=MESH
        )

    def rows_copy(p, owner):
        return to_core(mod_rows.at[p, owner], p)

    def other_copy(p, owner):
        return to_core(mod_other.at[p, owner], 16 + p)

    def to_chip(src, dst, i):
        return pltpu.make_async_remote_copy(
            src_ref=src, dst_ref=dst, send_sem=x_s.at[i], recv_sem=x_r.at[i], device_id=G.dev(dx=1), device_id_type=MESH
        )

    def lend(p):
        return to_chip(mod_rows.at[p, me], mod_other.at[p, me], p)

    def give_back(s, p):
        return to_chip(qkv_out.at[s, p], qkv_in.at[s, p], 4 + 4 * s + p)

    def mixed_copy(p, owner):
        return to_core(mixed.at[owner, p], 4 + p)

    def att_copy(j, p, owner):
        return to_core(att.at[owner, j, p, 1 - owner], 8 + 4 * j + p)

    def hand_over(j, p, cc):
        cols = pl.ds(cc * 1536 + j * 768, 768)
        i = 8 * j + 2 * p + cc
        return pltpu.make_async_remote_copy(
            src_ref=rows_out.at[p, :, cols],
            dst_ref=came.at[p, :, cols],
            send_sem=sec_s.at[i],
            recv_sem=sec_r.at[i],
            device_id={"section": 1 - sec},
            device_id_type=MESH,
        )

    def rows_done(p):
        return pltpu.make_async_copy(rows_out.at[p], out_ref.at[p], done_sem.at[p])

    def modulate(x, p):
        rows = x[p].astype(F32)
        mean = jnp.mean(rows, -1, keepdims=True)
        cent = rows - mean
        var = jnp.mean(jnp.square(cent), -1, keepdims=True)
        mod_rows[p, me] = (
            cent * lax.rsqrt(var + EPS) * (1.0 + mod_ref[1:2]) + mod_ref[0:1]
        ).astype(BF16)

    def by_head():
        table.wait()

        def one(i, carry):
            at = pl.ds(pl.multiple_of(128 + i * 64, 64), 64)
            for t in range(2):
                kv[:, t, at] = jnp.swapaxes(raw[at, t].astype(F32), 0, 1).astype(BF16)
            return carry

        lax.fori_loop(0, 6, one, 0)

        def turn(h, carry):
            keys[h, :, 128:512] = kv[h, 0, 128:512].astype(F32).T.astype(BF16)
            return carry

        lax.fori_loop(0, 8, turn, 0)

    def table_done(p):
        at = pl.ds(p * 128, 128)
        return pltpu.make_async_copy(raw.at[at], kv_out_ref.at[at], done_sem.at[4 + p])

    def by_token(p):
        for half in range(2):
            at = slice(p * 128 + half * 64, p * 128 + half * 64 + 64)
            for t in range(2):
                raw[at, t] = jnp.swapaxes(kv[:, t, at].astype(F32), 0, 1).astype(BF16)
        table_done(p).start()

    def normed(a):
        return (a * lax.rsqrt(jnp.mean(jnp.square(a), -1, keepdims=True) + EPS)).astype(BF16)

    def qkv(s, m):
        def part(t):
            w = gq[s, :, :, :, :, t * 256 : (t + 1) * 256].reshape(3072, 256)
            return jnp.dot(m, w, preferred_element_type=F32)

        return part(0), part(1), part(2)

    def attend(pair, p, parts):
        at = slice(p * 128, (p + 1) * 128)
        for hh, (_, k, v) in enumerate(parts):
            kv[2 * pair + hh, 0, at] = k
            keys[2 * pair + hh, :, at] = k.astype(F32).T.astype(BF16)
            kv[2 * pair + hh, 1, at] = v
        scores = [
            jnp.dot(q, keys[2 * pair + hh], preferred_element_type=F32)
            for hh, (q, _, _) in enumerate(parts)
        ]
        weights = [jnp.exp2(a * (math.log2(math.e) / math.sqrt(128.0))).astype(BF16) for a in scores]
        ones = jnp.ones((512, 128), BF16)
        sums = [
            jnp.dot(
                e, jnp.concatenate([kv[2 * pair + hh, 1], ones], 1), preferred_element_type=F32
            )
            for hh, e in enumerate(weights)
        ]
        mixed[me, p, :, pl.ds(pl.multiple_of(pair * 256, 256), 256)] = jnp.concatenate(
            [a[:, :128] / a[:, 128:] for a in sums], 1
        ).astype(BF16)

    def heads(s, pair, p0, np_):
        m = mod_rows[p0 : p0 + np_].reshape(np_ * 128, 3072)
        q2, k2, v2 = qkv(s, m)
        parts = []
        for hh in range(2):
            cols = slice(hh * 128, (hh + 1) * 128)
            parts.append((normed(q2[:, cols]), normed(k2[:, cols]), v2[:, cols].astype(BF16)))
        for i in range(np_):
            here = slice(i * 128, (i + 1) * 128)
            attend(pair, p0 + i, [tuple(a[here] for a in part) for part in parts])

    def qkv_other(s):
        q2, k2, v2 = qkv(s, mod_other[...].reshape(512, 3072))
        for hh in range(2):
            cols = slice(hh * 128, (hh + 1) * 128)
            parts = (normed(q2[:, cols]), normed(k2[:, cols]), v2[:, cols].astype(BF16))
            for t, part in enumerate(parts):
                qkv_out[s, :, :, t * 256 + hh * 128 : t * 256 + (hh + 1) * 128] = part.reshape(4, 128, 128)
        for p in range(4):
            give_back(s, p).start()

    def attend_back(s, p):
        give_back(s, p).wait_recv()
        parts = [
            tuple(qkv_in[s, p, :, t * 256 + hh * 128 : t * 256 + (hh + 1) * 128] for t in range(3))
            for hh in range(2)
        ]
        attend(2 * (1 - G.x) + s, p, parts)

    def columns(j, p0, np_):
        n = np_ * 128
        total = None
        for cc in range(2):
            a = mixed[cc, p0 : p0 + np_].reshape(n, 1024)
            w = go[j, 2 * cc : 2 * cc + 2].reshape(1024, 768)
            term = jnp.dot(a, w, preferred_element_type=F32)
            total = term if total is None else total + term
        att[me, j, p0 : p0 + np_] = total.astype(BF16).reshape(np_, 2, 64, 768)
        for p in range(p0, p0 + np_):
            att_copy(j, p, me).start()

    def finish(x, j, p):
        att_copy(j, p, 1 - me).wait_recv()
        for cc in range(2):
            cols = slice(cc * 1536 + j * 768, cc * 1536 + (j + 1) * 768)
            rows_out[p, :, cols] = (
                x[p, :, cols].astype(F32) + mod_ref[2:3, cols] * att[cc, j, p, me].astype(F32)
            ).astype(BF16)

    stages = [("q", s) for s in range(4)] + [("o0", 0), ("o1", 1)]
    halves = [("q", 0), ("q", 1), ("o", 0), ("o", 1)]

    @pl.when(first)
    def _():
        q0, q1, o0, o1 = halves

        def lent(p):
            lend(p).wait_recv()
            other_copy(p, me).start()

        H.t0(q0)
        for c in half_q:
            c.start()
        H.t0(q1)
        H.t0(o0)
        for p in range(2):
            modulate(x_ref, p)
            lend(p).start()
            rows_copy(p, me).start()
        for c in half_q + own_o:
            c.wait()
        H.t1(q0)
        for p in range(2, 4):
            modulate(x_ref, p)
            rows_copy(p, me).start()
        H.t2(q0)
        H.t1(q1)
        H.t3(q0)
        H.t2(q1)
        lent(0)
        lend(2).start()
        H.t4(q0)
        H.t3(q1)
        lent(1)
        lend(3).start()
        H.t5(q0)
        H.t1(o0)
        H.t0(o1)
        lent(2)
        by_head()
        for p in range(4):
            rows_copy(p, 1 - me).wait_recv()
        lent(3)
        for p in range(4):
            other_copy(p, 1 - me).wait_recv()
        qkv_other(0)
        H.t1(o1)
        H.t2(o0)
        H.t4(q1)
        H.t2(o1)
        heads(0, 2 * G.x, 0, 4)
        H.t3(o0)
        H.t5(q1)
        H.t3(o1)
        qkv_other(1)
        H.t4(o0)
        heads(1, 2 * G.x + 1, 0, 4)
        H.t4(o1)
        for p in range(4):
            attend_back(0, p)

        def hand(n):
            j, p = PIECES[n]
            finish(x_ref, j, p)
            for cc in range(2):
                if n >= 2:
                    hand_over(*PIECES[n - 2], cc).wait_send()
                hand_over(j, p, cc).start()
            if j == 1:
                rows_done(p).start()
                by_token(p)

        for p in range(5):
            if p < 4:
                attend_back(1, p)
                mixed_copy(p, me).start()
            if p == 1:
                H.t5(o0)
            if p > 0:
                mixed_copy(p - 1, 1 - me).wait_recv()
                columns(0, p - 1, 1)
            if p in (2, 3):
                hand(p - 2)
        H.t5(o1)
        for p in range(4):
            columns(1, p, 1)
            if p > 0:
                hand(p + 1)
        for n in range(5, 8):
            hand(n)

    @pl.when(jnp.logical_not(first))
    def _():
        for c in own_q:
            c.start()
        for c in own_q + own_o:
            c.wait()
        G.t0(stages[0])
        G.t0(stages[1])
        by_head()
        for i in range(7):
            G.tick(i, stages)
        G.ab3(stages[5])
        G.cd4(stages[5])
        G.ab4(stages[4])
        G.ab4(stages[5])

        def rows_in(p):
            for j in range(2):
                for cc in range(2):
                    hand_over(j, p, cc).wait_recv()
            modulate(came, p)
            rows_copy(p, me).start()

        def all_columns(p):
            mixed_copy(p, 1 - me).wait_recv()
            for j in range(2):
                columns(j, p, 1)

        def all_finish(p):
            for j in range(2):
                finish(came, j, p)
            rows_done(p).start()

        for p in range(4):
            rows_in(p)
            if p == 2:
                G.t5(stages[4])
                G.t5(stages[5])
                all_columns(0)
            if p > 1:
                all_columns(p - 1)
            rows_copy(p, 1 - me).wait_recv()

            def one(s, carry):
                if p == 0:

                    @pl.when(s == 3)
                    def _():
                        G.t5(stages[3])

                heads(s, s, p, 1)
                return carry

            lax.fori_loop(0, 4, one, 0)
            mixed_copy(p, me).start()
            by_token(p)
            if p == 2:
                all_finish(0)
            if p > 1:
                all_finish(p - 1)
        all_columns(3)
        all_finish(3)

    for p in range(4):
        rows_done(p).wait()
        table_done(p).wait()
        rows_copy(p, me).wait_send()
        for j in range(2):
            att_copy(j, p, me).wait_send()

    @pl.when(first)
    def _():
        for s in halves:
            H.sent(s)
        for p in range(4):
            lend(p).wait_send()
            other_copy(p, me).wait_send()
            mixed_copy(p, me).wait_send()
            for j in range(2):
                give_back(j, p).wait_send()
        for n in (6, 7):
            for cc in range(2):
                hand_over(*PIECES[n], cc).wait_send()

    @pl.when(jnp.logical_not(first))
    def _():
        for s in stages:
            G.sent(s)
        for p in range(4):
            mixed_copy(p, me).wait_send()


def local(x_in, time_index, mod_table, w_qkv, w_out, stale_kv):
    modulation = lax.dynamic_index_in_dim(mod_table[0], time_index[0], 0, keepdims=False)
    wq = w_qkv[0].reshape(96, 4, 2, 3, 128).transpose(1, 0, 3, 2, 4).reshape(4, 96, 768)
    anywhere = pl.BlockSpec(memory_space=pl.ANY)
    vmem = pl.BlockSpec(memory_space=pltpu.VMEM)
    dma = pltpu.SemaphoreType.DMA
    rows, kv = pl.pallas_call(
        kernel,
        in_specs=[vmem, vmem, anywhere, anywhere, anywhere],
        out_specs=(anywhere, anywhere),
        out_shape=(
            jax.ShapeDtypeStruct((4, 64, 3072), BF16),
            jax.ShapeDtypeStruct((512, 2, 8, 128), BF16),
        ),
        scratch_shapes=[
            pltpu.VMEM((4, 4, 4, 2, 96, 768), BF16),
            pltpu.VMEM((2, 4, 4, 2, 64, 768), BF16),
            pltpu.VMEM((4, 2, 64, 3072), BF16),
            pltpu.VMEM((2, 4, 128, 1024), BF16),
            pltpu.VMEM((2, 2, 4, 2, 64, 768), BF16),
            pltpu.VMEM((4, 64, 3072), BF16),
            pltpu.VMEM((4, 64, 3072), BF16),
            pltpu.VMEM((8, 2, 512, 128), BF16),
            pltpu.VMEM((4, 2, 64, 3072), BF16),
            pltpu.VMEM((2, 4, 128, 768), BF16),
            pltpu.VMEM((2, 4, 128, 768), BF16),
            pltpu.VMEM((512, 2, 8, 128), BF16),
            pltpu.VMEM((8, 128, 512), BF16),
            dma((6 * SEMS,)),
            dma((6 * SEMS,)),
            dma((7,)),
            dma((20,)),
            dma((20,)),
            dma((16,)),
            dma((16,)),
            dma((12,)),
            dma((12,)),
            dma((8,)),
        ],
        compiler_params=pltpu.CompilerParams(
            collective_id=0, has_side_effects=True, vmem_limit_bytes=60 * 2**20
        ),
        cost_estimate=pl.CostEstimate(flops=14 * 10**9, bytes_accessed=10**7, transcendentals=2 * 10**6),
        name="two_blocks",
    )(x_in[0], modulation, wq, w_out[0], stale_kv[0, 0])
    return rows[None, None], kv[None, None]


def solution(mesh):
    placed = (
        P("dp", None, "seq", None),
        P("dp"),
        P("section", None, None, None),
        P("section", "dp", "seq", None, None),
        P("section", "dp", "seq"),
        P("section", "dp", None, None, "seq", None),
    )
    return jax.shard_map(
        local,
        mesh=mesh,
        in_specs=placed,
        out_specs=(
            P("section", "dp", None, "seq", None),
            P("section", "dp", None, None, "seq", None),
        ),
        check_vma=False,
    )
```

```python
import functools
import math

import jax
import jax.numpy as jnp
from jax import lax
from jax.experimental import pallas as pl
from jax.experimental.pallas import tpu as pltpu
from jax.sharding import PartitionSpec as P

EPS = 1e-06
PIECES = ((0, 0), (0, 1), (1, 0), (1, 1), (0, 2), (1, 2), (0, 3), (1, 3))
MESH = pl.DeviceIdType.MESH
ALL = slice(None)
BF16 = jnp.bfloat16
F32 = jnp.float32

ROWS = {
    "q": {"A": (0, 32), "B": (32, 32), "C": (64, 16), "D": (80, 16)},
    "o0": {"A": (0, 32), "B": (32, 16), "C": (48, 16)},
    "o1": {"A": (0, 16), "B": (16, 32), "D": (48, 16)},
}
SEMS = 34
FIRST = {"q": 0, "o0": 4 * SEMS, "o1": 5 * SEMS}
PART = {"A": 0, "B": 9, "C": 18, "D": 26}


class Gather:
    def __init__(self, gq, go, ssem, rsem):
        dp = lax.axis_index("dp")
        self.z, self.y, self.x = lax.div(dp, 8), lax.rem(lax.div(dp, 2), 4), lax.rem(dp, 2)
        self.gq, self.go, self.ssem, self.rsem = gq, go, ssem, rsem
        self.r = {part: self.ring(part in "BD", part) for part in "ABCD"}

    def step(self, v, by):
        return lax.rem(v + (by + 4), 4)

    def dev(self, dz=0, dy=0, dx=0):
        z = self.step(self.z, dz) if dz else self.z
        y = self.step(self.y, dy) if dy else self.y
        x = 1 - self.x if dx else self.x
        return {"dp": z * 8 + y * 2 + x}

    def copy(self, stage, part, k, sel, to):
        kind, s = stage
        r0, n = ROWS[kind][part]
        rows = pl.ds(r0, n)
        if kind == "q":
            v = self.gq.at[(s, *sel, rows, ALL)]
        else:
            v = self.go.at[(s, *sel, rows, ALL)]
        i = FIRST[kind] + (s * SEMS if kind == "q" else 0) + PART[part] + k
        return pltpu.make_async_remote_copy(
            src_ref=v,
            dst_ref=v,
            send_sem=self.ssem.at[i],
            recv_sem=self.rsem.at[i],
            device_id=to,
            device_id_type=MESH,
        )

    def ring(self, swap, part):
        f0, g0 = (self.z, self.y) if swap else (self.y, self.z)
        st, x = self.step, self.x

        def sel(f, g, xs):
            return (f, g, xs) if swap else (g, f, xs)

        def to(df=0, dg=0, dx=0):
            return self.dev(dz=df, dy=dg, dx=dx) if swap else self.dev(dz=dg, dy=df, dx=dx)

        low, high = pl.ds(0, 2), pl.ds(2, 2)
        if part in "AB":
            return [
                (sel(f0, g0, x), sel(f0, g0, 1 - x), to(dx=1)),
                (sel(f0, g0, ALL), sel(st(f0, -1), g0, ALL), to(df=1)),
                (sel(f0, g0, ALL), sel(st(f0, 1), g0, ALL), to(df=-1)),
                (sel(st(f0, -1), g0, 0), sel(st(f0, 2), g0, 0), to(df=1)),
                (sel(st(f0, 1), g0, 1), sel(st(f0, 2), g0, 1), to(df=-1)),
                (sel(ALL, g0, ALL), sel(ALL, st(g0, -1), ALL), to(dg=1)),
                (sel(ALL, g0, ALL), sel(ALL, st(g0, 1), ALL), to(dg=-1)),
                (sel(low, st(g0, -1), ALL), sel(low, st(g0, 2), ALL), to(dg=1)),
                (sel(high, st(g0, 1), ALL), sel(high, st(g0, 2), ALL), to(dg=-1)),
            ]
        sg = 1 if part == "C" else -1
        return [
            (sel(f0, g0, x), sel(st(f0, -1), g0, x), to(df=1)),
            (sel(f0, g0, x), sel(st(f0, 1), g0, x), to(df=-1)),
            (sel(st(f0, -sg), g0, x), sel(st(f0, 2), g0, x), to(df=sg)),
            (sel(ALL, g0, x), sel(ALL, st(g0, -1), x), to(dg=1)),
            (sel(ALL, g0, x), sel(ALL, st(g0, 1), x), to(dg=-1)),
            (sel(low, st(g0, -1), x), sel(low, st(g0, 2), x), to(dg=1)),
            (sel(high, st(g0, 1), x), sel(high, st(g0, 2), x), to(dg=-1)),
            (sel(ALL, ALL, x), sel(ALL, ALL, 1 - x), to(dx=1)),
        ]

    def start(self, stage, part, *ks):
        if part in ROWS[stage[0]]:
            for k in ks:
                out, _, to = self.r[part][k]
                self.copy(stage, part, k, out, to).start()

    def got(self, stage, part, *ks):
        if part in ROWS[stage[0]]:
            for k in ks:
                _, came, to = self.r[part][k]
                self.copy(stage, part, k, came, to).wait_recv()

    def sent(self, stage):
        for part in ROWS[stage[0]]:
            for k, (out, _, to) in enumerate(self.r[part]):
                self.copy(stage, part, k, out, to).wait_send()

    def t0(self, s):
        for p in "CD":
            self.start(s, p, 0, 1)
        for p in "AB":
            self.start(s, p, 0)

    def cd1(self, s):
        for p, k in (("C", 0), ("D", 1)):
            self.got(s, p, k)
            self.start(s, p, 2)

    def ab1(self, s):
        for p in "AB":
            self.got(s, p, 0)
            self.start(s, p, 1, 2)

    def cd2(self, s):
        for p, k in (("C", 1), ("D", 0)):
            self.got(s, p, k, 2)
            self.start(s, p, 3, 4)

    def ab2(self, s):
        for p in "AB":
            self.got(s, p, 1)
            self.start(s, p, 3)
            self.got(s, p, 2)
            self.start(s, p, 4)

    def cd3(self, s):
        for p in "CD":
            self.got(s, p, 3)
            self.start(s, p, 5)
            self.got(s, p, 4)
            self.start(s, p, 6)

    def ab3(self, s):
        for p in "AB":
            self.got(s, p, 3, 4)
            self.start(s, p, 5, 6)

    def cd4(self, s):
        for p in "CD":
            self.got(s, p, 5, 6)
            self.start(s, p, 7)

    def ab4(self, s):
        for p in "AB":
            self.got(s, p, 5)
            self.start(s, p, 7)
            self.got(s, p, 6)
            self.start(s, p, 8)

    def t5(self, s):
        for p in "AB":
            self.got(s, p, 7, 8)
        for p in "CD":
            self.got(s, p, 7)

    def tick(self, i, stages):
        for step, lag in (
            (self.cd1, 0),
            (self.cd2, 1),
            (self.t0, -2),
            (self.ab1, 0),
            (self.ab2, 1),
            (self.ab3, 2),
            (self.cd3, 1),
            (self.cd4, 2),
            (self.ab4, 3),
            (self.t5, 4),
        ):
            if 0 <= i - lag < len(stages):
                step(stages[i - lag])


class HalfGather(Gather):
    SPLIT = {"q": 48, "o": 32}

    def __init__(self, wq, wo, *rest):
        super().__init__(*rest)
        self.wq, self.wo = wq, wo

    def copy(self, stage, part, k, sel, to):
        kind, s = stage
        n = self.SPLIT[kind]
        i = ((0 if kind == "q" else 2) + s) * 18 + PART[part] + k
        rows = pl.ds(0 if part == "A" else n, n)
        buf = self.gq if kind == "q" else self.go
        if k == 0:
            v = buf.at[(s, *sel, ALL, ALL)]
            src = self.wq.at[2 * (1 - self.x) + s] if kind == "q" else self.wo.at[:, pl.ds(768 * s, 768)]
        else:
            v = src = buf.at[(s, *sel, rows, ALL)]
        return pltpu.make_async_remote_copy(
            src_ref=src,
            dst_ref=v,
            send_sem=self.ssem.at[i],
            recv_sem=self.rsem.at[i],
            device_id=to,
            device_id_type=MESH,
        )

    def start(self, stage, part, *ks):
        for k in ks:
            out, _, to = self.r[part][k]
            self.copy(stage, part, k, out, to).start()

    def got(self, stage, part, *ks):
        for k in ks:
            _, came, to = self.r[part][k]
            self.copy(stage, part, k, came, to).wait_recv()

    def sent(self, stage):
        for part in "AB":
            for k in range(0 if part == "A" else 1, 9):
                out, _, to = self.r[part][k]
                self.copy(stage, part, k, out, to).wait_send()

    def t0(self, s):
        self.start(s, "A", 0)

    def t1(self, s):
        self.got(s, "A", 0)
        for p in "AB":
            self.start(s, p, 1, 2)

    t2, t3, t4 = Gather.ab2, Gather.ab3, Gather.ab4

    def t5(self, s):
        for p in "AB":
            self.got(s, p, 7, 8)


def kernel(
    x_ref,
    mod_ref,
    wq_ref,
    wo_ref,
    stale_ref,
    out_ref,
    kv_out_ref,
    gq,
    go,
    mod_rows,
    mixed,
    att,
    came,
    rows_out,
    kv,
    mod_other,
    qkv_out,
    qkv_in,
    raw,
    keys,
    ssem,
    rsem,
    lsem,
    core_s,
    core_r,
    sec_s,
    sec_r,
    x_s,
    x_r,
    done_sem,
):
    sec, me = lax.axis_index("section"), lax.axis_index("seq")
    first = sec == 0
    other = {"seq": 1 - me}
    G = Gather(gq, go, ssem, rsem)
    H = HalfGather(wq_ref, wo_ref, gq, go, ssem, rsem)
    own_q = [pltpu.make_async_copy(wq_ref.at[i], gq.at[i, G.z, G.y, G.x], lsem.at[i]) for i in range(4)]
    half_q = [
        pltpu.make_async_copy(wq_ref.at[2 * G.x + i], gq.at[i, G.z, G.y, G.x], lsem.at[i])
        for i in range(2)
    ]
    own_o = [
        pltpu.make_async_copy(
            wo_ref.at[:, pl.ds(768 * i, 768)], go.at[i, G.z, G.y, G.x], lsem.at[4 + i]
        )
        for i in range(2)
    ]
    table = pltpu.make_async_copy(stale_ref, raw, lsem.at[6])
    for c in own_o:
        c.start()
    table.start()
    barrier = pltpu.get_barrier_semaphore()
    for to in (
        G.dev(dz=1), G.dev(dz=-1), G.dev(dy=1), G.dev(dy=-1), G.dev(dx=1), other, {"section": 1 - sec},
    ):
        pl.semaphore_signal(barrier, inc=1, device_id=to, device_id_type=MESH)
    pl.semaphore_wait(barrier, 7)

    def to_core(v, i):
        return pltpu.make_async_remote_copy(
            src_ref=v, dst_ref=v, send_sem=core_s.at[i], recv_sem=core_r.at[i], device_id=other, device_id_type=MESH
        )

    def rows_copy(p, owner):
        return to_core(mod_rows.at[p, owner], p)

    def other_copy(p, owner):
        return to_core(mod_other.at[p, owner], 16 + p)

    def to_chip(src, dst, i):
        return pltpu.make_async_remote_copy(
            src_ref=src, dst_ref=dst, send_sem=x_s.at[i], recv_sem=x_r.at[i], device_id=G.dev(dx=1), device_id_type=MESH
        )

    def lend(p):
        return to_chip(mod_rows.at[p, me], mod_other.at[p, me], p)

    def give_back(s, p):
        return to_chip(qkv_out.at[s, p], qkv_in.at[s, p], 4 + 4 * s + p)

    def mixed_copy(p, owner):
        return to_core(mixed.at[owner, p], 4 + p)

    def att_copy(j, p, owner):
        return to_core(att.at[owner, j, p, 1 - owner], 8 + 4 * j + p)

    def hand_over(j, p, cc):
        cols = pl.ds(cc * 1536 + j * 768, 768)
        i = 8 * j + 2 * p + cc
        return pltpu.make_async_remote_copy(
            src_ref=rows_out.at[p, :, cols],
            dst_ref=came.at[p, :, cols],
            send_sem=sec_s.at[i],
            recv_sem=sec_r.at[i],
            device_id={"section": 1 - sec},
            device_id_type=MESH,
        )

    def rows_done(p):
        return pltpu.make_async_copy(rows_out.at[p], out_ref.at[p], done_sem.at[p])

    def modulate(x, p):
        rows = x[p].astype(F32)
        mean = jnp.mean(rows, -1, keepdims=True)
        cent = rows - mean
        var = jnp.mean(jnp.square(cent), -1, keepdims=True)
        mod_rows[p, me] = (
            cent * lax.rsqrt(var + EPS) * (1.0 + mod_ref[1:2]) + mod_ref[0:1]
        ).astype(BF16)

    def by_head():
        table.wait()

        def one(i, carry):
            at = pl.ds(pl.multiple_of(128 + i * 64, 64), 64)
            for t in range(2):
                kv[:, t, at] = jnp.swapaxes(raw[at, t].astype(F32), 0, 1).astype(BF16)
            return carry

        lax.fori_loop(0, 6, one, 0)

        def turn(h, carry):
            keys[h, :, 128:512] = kv[h, 0, 128:512].astype(F32).T.astype(BF16)
            return carry

        lax.fori_loop(0, 8, turn, 0)

    def table_done(p):
        at = pl.ds(p * 128, 128)
        return pltpu.make_async_copy(raw.at[at], kv_out_ref.at[at], done_sem.at[4 + p])

    def by_token(p):
        for half in range(2):
            at = slice(p * 128 + half * 64, p * 128 + half * 64 + 64)
            for t in range(2):
                raw[at, t] = jnp.swapaxes(kv[:, t, at].astype(F32), 0, 1).astype(BF16)
        table_done(p).start()

    def normed(a):
        return (a * lax.rsqrt(jnp.mean(jnp.square(a), -1, keepdims=True) + EPS)).astype(BF16)

    def qkv(s, m):
        def part(t):
            w = gq[s, :, :, :, :, t * 256 : (t + 1) * 256].reshape(3072, 256)
            return jnp.dot(m, w, preferred_element_type=F32)

        return part(0), part(1), part(2)

    def attend(pair, p, parts):
        at = slice(p * 128, (p + 1) * 128)
        for hh, (_, k, v) in enumerate(parts):
            kv[2 * pair + hh, 0, at] = k
            keys[2 * pair + hh, :, at] = k.astype(F32).T.astype(BF16)
            kv[2 * pair + hh, 1, at] = v
        scores = [
            jnp.dot(q, keys[2 * pair + hh], preferred_element_type=F32)
            for hh, (q, _, _) in enumerate(parts)
        ]
        weights = [jnp.exp2(a * (math.log2(math.e) / math.sqrt(128.0))).astype(BF16) for a in scores]
        ones = jnp.ones((512, 128), BF16)
        sums = [
            jnp.dot(
                e, jnp.concatenate([kv[2 * pair + hh, 1], ones], 1), preferred_element_type=F32
            )
            for hh, e in enumerate(weights)
        ]
        mixed[me, p, :, pl.ds(pl.multiple_of(pair * 256, 256), 256)] = jnp.concatenate(
            [a[:, :128] / a[:, 128:] for a in sums], 1
        ).astype(BF16)

    def heads(s, pair, p0, np_):
        m = mod_rows[p0 : p0 + np_].reshape(np_ * 128, 3072)
        q2, k2, v2 = qkv(s, m)
        parts = []
        for hh in range(2):
            cols = slice(hh * 128, (hh + 1) * 128)
            parts.append((normed(q2[:, cols]), normed(k2[:, cols]), v2[:, cols].astype(BF16)))
        for i in range(np_):
            here = slice(i * 128, (i + 1) * 128)
            attend(pair, p0 + i, [tuple(a[here] for a in part) for part in parts])

    def qkv_other(s):
        q2, k2, v2 = qkv(s, mod_other[...].reshape(512, 3072))
        for hh in range(2):
            cols = slice(hh * 128, (hh + 1) * 128)
            parts = (normed(q2[:, cols]), normed(k2[:, cols]), v2[:, cols].astype(BF16))
            for t, part in enumerate(parts):
                qkv_out[s, :, :, t * 256 + hh * 128 : t * 256 + (hh + 1) * 128] = part.reshape(4, 128, 128)
        for p in range(4):
            give_back(s, p).start()

    def attend_back(s, p):
        give_back(s, p).wait_recv()
        parts = [
            tuple(qkv_in[s, p, :, t * 256 + hh * 128 : t * 256 + (hh + 1) * 128] for t in range(3))
            for hh in range(2)
        ]
        attend(2 * (1 - G.x) + s, p, parts)

    def columns(j, p0, np_):
        n = np_ * 128
        total = None
        for cc in range(2):
            a = mixed[cc, p0 : p0 + np_].reshape(n, 1024)
            w = go[j, 2 * cc : 2 * cc + 2].reshape(1024, 768)
            term = jnp.dot(a, w, preferred_element_type=F32)
            total = term if total is None else total + term
        att[me, j, p0 : p0 + np_] = total.astype(BF16).reshape(np_, 2, 64, 768)
        for p in range(p0, p0 + np_):
            att_copy(j, p, me).start()

    def finish(x, j, p):
        att_copy(j, p, 1 - me).wait_recv()
        for cc in range(2):
            cols = slice(cc * 1536 + j * 768, cc * 1536 + (j + 1) * 768)
            rows_out[p, :, cols] = (
                x[p, :, cols].astype(F32) + mod_ref[2:3, cols] * att[cc, j, p, me].astype(F32)
            ).astype(BF16)

    stages = [("q", s) for s in range(4)] + [("o0", 0), ("o1", 1)]
    halves = [("q", 0), ("q", 1), ("o", 0), ("o", 1)]

    @pl.when(first)
    def _():
        q0, q1, o0, o1 = halves

        def lent(p):
            lend(p).wait_recv()
            other_copy(p, me).start()

        H.t0(q0)
        for c in half_q:
            c.start()
        H.t0(q1)
        H.t0(o0)
        for p in range(2):
            modulate(x_ref, p)
            lend(p).start()
            rows_copy(p, me).start()
        for c in half_q + own_o:
            c.wait()
        H.t1(q0)
        for p in range(2, 4):
            modulate(x_ref, p)
            rows_copy(p, me).start()
        H.t2(q0)
        H.t1(q1)
        H.t3(q0)
        H.t2(q1)
        lent(0)
        lend(2).start()
        H.t4(q0)
        H.t3(q1)
        lent(1)
        lend(3).start()
        H.t5(q0)
        H.t1(o0)
        H.t0(o1)
        lent(2)
        by_head()
        for p in range(4):
            rows_copy(p, 1 - me).wait_recv()
        lent(3)
        for p in range(4):
            other_copy(p, 1 - me).wait_recv()
        qkv_other(0)
        H.t1(o1)
        H.t2(o0)
        H.t4(q1)
        H.t2(o1)
        heads(0, 2 * G.x, 0, 4)
        H.t3(o0)
        H.t5(q1)
        H.t3(o1)
        qkv_other(1)
        H.t4(o0)
        heads(1, 2 * G.x + 1, 0, 4)
        H.t4(o1)
        for p in range(4):
            attend_back(0, p)

        def hand(n):
            j, p = PIECES[n]
            finish(x_ref, j, p)
            for cc in range(2):
                if n >= 2:
                    hand_over(*PIECES[n - 2], cc).wait_send()
                hand_over(j, p, cc).start()
            if j == 1:
                rows_done(p).start()
                by_token(p)

        for p in range(5):
            if p < 4:
                attend_back(1, p)
                mixed_copy(p, me).start()
            if p == 1:
                H.t5(o0)
            if p > 0:
                mixed_copy(p - 1, 1 - me).wait_recv()
                columns(0, p - 1, 1)
            if p in (2, 3):
                hand(p - 2)
        H.t5(o1)
        for p in range(4):
            columns(1, p, 1)
            if p > 0:
                hand(p + 1)
        for n in range(5, 8):
            hand(n)

    @pl.when(jnp.logical_not(first))
    def _():
        for c in own_q:
            c.start()
        for c in own_q + own_o:
            c.wait()
        G.t0(stages[0])
        G.t0(stages[1])
        by_head()
        for i in range(7):
            G.tick(i, stages)
            if i > 4:
                G.sent(stages[i - 5])
        G.ab3(stages[5])
        G.cd4(stages[5])
        G.ab4(stages[4])
        G.sent(stages[2])
        G.ab4(stages[5])

        def rows_in(p):
            for j in range(2):
                for cc in range(2):
                    hand_over(j, p, cc).wait_recv()
            modulate(came, p)
            rows_copy(p, me).start()

        def all_columns(p):
            mixed_copy(p, 1 - me).wait_recv()
            for j in range(2):
                columns(j, p, 1)

        def all_finish(p):
            for j in range(2):
                finish(came, j, p)
            rows_done(p).start()

        for p in range(4):
            if p == 3:
                for s in stages[3:]:
                    G.sent(s)
            rows_in(p)
            if p == 2:
                G.t5(stages[4])
                G.t5(stages[5])
                all_columns(0)
            if p > 1:
                all_columns(p - 1)
            rows_copy(p, 1 - me).wait_recv()

            def one(s, carry):
                if p == 0:

                    @pl.when(s == 3)
                    def _():
                        G.t5(stages[3])

                heads(s, s, p, 1)
                return carry

            lax.fori_loop(0, 4, one, 0)
            mixed_copy(p, me).start()
            by_token(p)
            if p == 2:
                all_finish(0)
            if p > 1:
                all_finish(p - 1)
        all_columns(3)
        all_finish(3)

    for p in range(4):
        rows_done(p).wait()
        table_done(p).wait()
        rows_copy(p, me).wait_send()
        for j in range(2):
            att_copy(j, p, me).wait_send()

    @pl.when(first)
    def _():
        for s in halves:
            H.sent(s)
        for p in range(4):
            lend(p).wait_send()
            other_copy(p, me).wait_send()
            mixed_copy(p, me).wait_send()
            for j in range(2):
                give_back(j, p).wait_send()
        for n in (6, 7):
            for cc in range(2):
                hand_over(*PIECES[n], cc).wait_send()

    @pl.when(jnp.logical_not(first))
    def _():
        for p in range(4):
            mixed_copy(p, me).wait_send()


def local(x_in, time_index, mod_table, w_qkv, w_out, stale_kv):
    modulation = lax.dynamic_index_in_dim(mod_table[0], time_index[0], 0, keepdims=False)
    wq = w_qkv[0].reshape(96, 4, 2, 3, 128).transpose(1, 0, 3, 2, 4).reshape(4, 96, 768)
    anywhere = pl.BlockSpec(memory_space=pl.ANY)
    vmem = pl.BlockSpec(memory_space=pltpu.VMEM)
    dma = pltpu.SemaphoreType.DMA
    rows, kv = pl.pallas_call(
        kernel,
        in_specs=[vmem, vmem, anywhere, anywhere, anywhere],
        out_specs=(anywhere, anywhere),
        out_shape=(
            jax.ShapeDtypeStruct((4, 64, 3072), BF16),
            jax.ShapeDtypeStruct((512, 2, 8, 128), BF16),
        ),
        scratch_shapes=[
            pltpu.VMEM((4, 4, 4, 2, 96, 768), BF16),
            pltpu.VMEM((2, 4, 4, 2, 64, 768), BF16),
            pltpu.VMEM((4, 2, 64, 3072), BF16),
            pltpu.VMEM((2, 4, 128, 1024), BF16),
            pltpu.VMEM((2, 2, 4, 2, 64, 768), BF16),
            pltpu.VMEM((4, 64, 3072), BF16),
            pltpu.VMEM((4, 64, 3072), BF16),
            pltpu.VMEM((8, 2, 512, 128), BF16),
            pltpu.VMEM((4, 2, 64, 3072), BF16),
            pltpu.VMEM((2, 4, 128, 768), BF16),
            pltpu.VMEM((2, 4, 128, 768), BF16),
            pltpu.VMEM((512, 2, 8, 128), BF16),
            pltpu.VMEM((8, 128, 512), BF16),
            dma((6 * SEMS,)),
            dma((6 * SEMS,)),
            dma((7,)),
            dma((20,)),
            dma((20,)),
            dma((16,)),
            dma((16,)),
            dma((12,)),
            dma((12,)),
            dma((8,)),
        ],
        compiler_params=pltpu.CompilerParams(
            collective_id=0, has_side_effects=True, vmem_limit_bytes=60 * 2**20
        ),
        cost_estimate=pl.CostEstimate(flops=14 * 10**9, bytes_accessed=10**7, transcendentals=2 * 10**6),
        name="two_blocks",
    )(x_in[0], modulation, wq, w_out[0], stale_kv[0, 0])
    return rows[None, None], kv[None, None]


def solution(mesh):
    placed = (
        P("dp", None, "seq", None),
        P("dp"),
        P("section", None, None, None),
        P("section", "dp", "seq", None, None),
        P("section", "dp", "seq"),
        P("section", "dp", None, None, "seq", None),
    )
    return jax.shard_map(
        local,
        mesh=mesh,
        in_specs=placed,
        out_specs=(
            P("section", "dp", None, "seq", None),
            P("section", "dp", None, None, "seq", None),
        ),
        check_vma=False,
    )
```
